32 devices in a mesh: nodes: 8 (over z, y), mp: 4 (over x, core).
Axes of the slice: x: 2, y: 2, z: 4, core: 2. Of those that a mesh axis runs over, the one named last changes fastest.
Arguments:
- event_feats: bfloat16 [8192, 512], P('nodes'), may hold values from -6 to 6
- event_owner: int32 [8192, 1], P('nodes'), may hold values from 0 to 7; in each aligned block of 1024 rows (0 to 1023, 1024 to 2047, ...) at most 256 rows name the same one
- event_slot: int32 [8192], P('nodes'), may hold values from 0 to 255
- memory: bfloat16 [2048, 1024], P('nodes'), may hold values from -6 to 6
- w_msg_event: bfloat16 [512, 2048], P(None, 'mp'), may hold values from -0.25 to 0.25
- w_msg_state: bfloat16 [1024, 2048], P(None, 'mp'), may hold values from -0.1875 to 0.1875
- b_msg: float32 [2048], P('mp'), may hold values from -3 to 3
- w_msg_out: bfloat16 [2048, 1024], P('mp'), may hold values from -0.125 to 0.125
- b_out: float32 [1024], replicated, may hold values from -3 to 3
- w_input: bfloat16 [3, 1024, 1024], P(None, None, 'mp'), may hold values from -0.1875 to 0.1875
- w_hidden: bfloat16 [3, 1024, 1024], P(None, None, 'mp'), may hold values from -0.1875 to 0.1875
- b_input: float32 [3, 1024], P(None, 'mp'), may hold values from -3 to 3
- b_hidden: float32 [3, 1024], P(None, 'mp'), may hold values from -3 to 3
- state_slots: int32 [64, 32], P('nodes'), may hold values from 0 to 255
- neighbours: int32 [2048, 10], P('nodes'), may hold values from 0 to 255
- query_slots: int32 [2048], P('nodes'), may hold values from 0 to 255
- w_neigh: bfloat16 [1024, 1024], P('mp'), may hold values from -0.1875 to 0.1875
- w_self: bfloat16 [1024, 1024], P('mp'), may hold values from -0.1875 to 0.1875
- b_embed: float32 [1024], replicated, may hold values from -3 to 3
Outputs:
- new_memory: bfloat16 [2048, 1024], P('nodes', 'mp')
- embedding: bfloat16 [2048, 1024], P(('nodes', 'mp'))
The draws below stay inside these ranges and needn't reach their ends.
Inputs may be any that keep to these rules, and one draw needn't show every extreme that they name: `event_owner`: among the 1024 events of one block of events, at most 256 name the same owner, and in every draw some owner is named exactly 256 times by some block.
All inputs are finite; a program needn't handle non-finite values.
Results may differ from the reference program's by a relative error of at most 0.014.
Values may be sent and summed in bfloat16 or wider, within the bound.
A program may use at most 64 MiB of HBM per device.

```python
import math
import jax
import jax.numpy as jnp
import numpy as np
from jax import lax

DM = 1024
FEAT = 512
MH = 2048
NEIGH = 10
STATE_CAP = 32
E_DEV = 1024
M_DEV = 256
Q_DEV = 256
OWNERS = 8
CAP = 256
EVENTS = 8192
NODES = 2048
QUERIES = 2048
N_NODES = 8


def place_ends(entries, key, least, top_value):
    longest = entries.shape.index(max(entries.shape))
    spots = []
    for shift in (0, 1):
        where = [jax.random.randint(jax.random.fold_in(key, axis), (), 0, length) for axis, length in enumerate(entries.shape)]
        where[longest] = (where[longest] + shift) % entries.shape[longest]
        spots.append(tuple(where))
    return entries.at[spots[0]].set(least).at[spots[1]].set(top_value)


def levels(rng, dims, cuts, least, top_value):
    gain = 1.0
    for axis_at, shards_of in cuts:
        draws = jax.random.uniform(jax.random.fold_in(jax.random.fold_in(rng, 6), axis_at), (shards_of,), jnp.float32, least / len(cuts), top_value / len(cuts))
        gain = gain * jnp.repeat(jnp.exp(draws), dims[axis_at] // shards_of).reshape((-1,) + (1,) * (len(dims) - 1 - axis_at))
    return gain


def routed_block(stream_key, own, number, rows, count, top, reach, slope):
    sequence = jax.random.permutation(stream_key, count)
    packed, common = shares(count, rows * top, reach, slope, True), shares(count, rows * top, reach, slope, False)
    places = jnp.arange(count)

    def named(tallies, offset_by):
        used = int((tallies > 0).sum())
        fixed = max(1, used // 4)
        passed = fixed + (places - fixed + offset_by * (used - fixed)) % max(1, count - fixed)
        return jnp.zeros((count,), jnp.int32).at[sequence[jnp.where(places < fixed, places, passed)]].set(jnp.asarray(tallies, jnp.int32))

    tallies = jnp.where(number % 4 == 0, named(packed, number // 4), named(common, number - number // 4 - 1))
    mixed = jax.random.permutation(jax.random.fold_in(own, 3), count)
    donor, receiver = mixed[0:count // 2 * 2:2], mixed[1:count // 2 * 2:2]
    room = jnp.minimum(tallies[donor] - 1, reach - tallies[receiver]) // 2
    room = jnp.where((donor == sequence[0]) | (receiver == sequence[0]) | (tallies[receiver] == 0), 0, jnp.maximum(room, 0))
    passed = jax.random.randint(jax.random.fold_in(own, 4), (count // 2,), 0, 1 << 20) % (room + 1)
    tallies = tallies.at[donor].add(-passed).at[receiver].add(passed)
    members = jnp.searchsorted(jnp.cumsum(tallies), jnp.arange(rows * top), side="right").astype(jnp.int32)
    grid = members.reshape(top, rows).T
    grid = grid[jax.random.permutation(jax.random.fold_in(own, 1), rows)]
    offset_by = jax.random.randint(jax.random.fold_in(own, 2), (rows, 1), 0, top)
    return jnp.take_along_axis(grid, (jnp.arange(top)[None, :] + offset_by) % top, axis=1)


def shares(number_of, total, most, slope, full):
    weights = [(1 << 20) // math.isqrt(standing ** slope) + 1 for standing in range(1, number_of + 1)]
    largest = most if full else min(most, max(-(-total // number_of), total * weights[0] // sum(weights)))
    least = 1 if total - largest >= number_of - 1 else 0
    holding, spare = [largest] + [least] * (number_of - 1), total - largest - least * (number_of - 1)
    while spare > 0:
        candidates = [i for i in range(1, number_of) if holding[i] < largest] or [i for i in range(1, number_of) if holding[i] < most]
        mass, remaining = sum([weights[i] for i in candidates]), spare
        for i in candidates:
            addition = min(most - holding[i], max(1, remaining * weights[i] // mass), spare)
            holding[i] = holding[i] + addition
            spare = spare - addition
    return np.array(holding)


def centred(stream_key, extent, scale, limit, shards=(), held_as=jnp.bfloat16):
    level = levels(stream_key, extent, shards, -0.22, 0.18) if shards else 1.0
    drawn = jax.random.normal(stream_key, extent, jnp.float32) * scale * level
    return jnp.minimum(jnp.maximum(drawn, -limit), limit).astype(held_as)


def setup_inputs(seed: int = 0) -> dict:
    seeds = jax.random.split(jax.random.key(seed), 20)
    event_feats = centred(seeds[0], (EVENTS, FEAT), 1.0, 6.0, ((0, 8),))
    event_owner_keys = jax.random.split(jax.random.fold_in(seeds[1], 1), EVENTS // E_DEV)
    event_owner_turns = jax.random.permutation(jax.random.fold_in(seeds[1], 3), EVENTS // E_DEV)
    event_owner = jax.vmap(lambda own, number: routed_block(jax.random.fold_in(seeds[1], 2), own, number, E_DEV, OWNERS, 1, CAP, 2))(event_owner_keys, event_owner_turns).reshape((EVENTS, 1))
    event_slot = place_ends(jax.random.randint(seeds[2], (EVENTS,), 0, M_DEV), jax.random.fold_in(seeds[2], 1), 0, M_DEV - 1).astype(jnp.int32)
    memory = centred(seeds[3], (NODES, DM), 1.0, 6.0, ((0, 8),))
    w_msg_event = centred(seeds[4], (FEAT, MH), FEAT ** -0.5, 0.25, ((1, 4),))
    w_msg_state = centred(seeds[5], (DM, MH), DM ** -0.5, 0.1875, ((1, 4),))
    b_msg = centred(seeds[6], (MH,), 0.5, 3.0, ((0, 4),), jnp.float32)
    w_msg_out = centred(seeds[7], (MH, DM), MH ** -0.5, 0.125, ((0, 4),))
    b_out = centred(seeds[8], (DM,), 0.5, 3.0, (), jnp.float32)
    w_input = centred(seeds[9], (3, DM, DM), DM ** -0.5, 0.1875, ((2, 4),))
    w_hidden = centred(seeds[10], (3, DM, DM), DM ** -0.5, 0.1875, ((2, 4),))
    b_input = centred(seeds[11], (3, DM), 0.5, 3.0, ((1, 4),), jnp.float32)
    b_hidden = centred(seeds[12], (3, DM), 0.5, 3.0, ((1, 4),), jnp.float32)
    state_slots = place_ends(jax.random.randint(seeds[13], (OWNERS * OWNERS, STATE_CAP), 0, M_DEV), jax.random.fold_in(seeds[13], 1), 0, M_DEV - 1).astype(jnp.int32)
    neighbours = place_ends(jax.random.randint(seeds[14], (QUERIES, NEIGH), 0, OWNERS * STATE_CAP), jax.random.fold_in(seeds[14], 1), 0, (OWNERS * STATE_CAP) - 1).astype(jnp.int32)
    query_slots = place_ends(jax.random.randint(seeds[15], (QUERIES,), 0, M_DEV), jax.random.fold_in(seeds[15], 1), 0, M_DEV - 1).astype(jnp.int32)
    w_neigh = centred(seeds[16], (DM, DM), DM ** -0.5, 0.1875, ((0, 4),))
    w_self = centred(seeds[17], (DM, DM), DM ** -0.5, 0.1875, ((0, 4),))
    b_embed = centred(seeds[18], (DM,), 0.5, 3.0, (), jnp.float32)
    return {"event_feats": event_feats, "event_owner": event_owner, "event_slot": event_slot, "memory": memory, "w_msg_event": w_msg_event, "w_msg_state": w_msg_state, "b_msg": b_msg, "w_msg_out": w_msg_out, "b_out": b_out, "w_input": w_input, "w_hidden": w_hidden, "b_input": b_input, "b_hidden": b_hidden, "state_slots": state_slots, "neighbours": neighbours, "query_slots": query_slots, "w_neigh": w_neigh, "w_self": w_self, "b_embed": b_embed}


def reference(event_feats, event_owner, event_slot, memory, w_msg_event, w_msg_state, b_msg, w_msg_out, b_out, w_input, w_hidden, b_input, b_hidden, state_slots, neighbours, query_slots, w_neigh, w_self, b_embed):
    dest = (event_owner[:, 0] * M_DEV + event_slot).astype(jnp.int32)
    state_proj = jnp.dot(memory, w_msg_state, preferred_element_type=jnp.float32)
    feats_blocks = event_feats.reshape(N_NODES, E_DEV, FEAT)
    dest_blocks = dest.reshape(N_NODES, E_DEV)

    def accumulate(carry, item):
        hidden_sum, counts = carry
        feats, targets = item
        pre = jnp.dot(feats, w_msg_event, preferred_element_type=jnp.float32) + state_proj[targets] + b_msg
        hidden_msg = jax.nn.relu(pre).astype(jnp.bfloat16)
        hidden_sum = hidden_sum.at[targets].add(hidden_msg.astype(jnp.float32))
        counts = counts.at[targets].add(jnp.ones((E_DEV,), jnp.float32))
        return (hidden_sum, counts), None

    start = (jnp.zeros((NODES, MH), jnp.float32), jnp.zeros((NODES,), jnp.float32))
    (hidden_sum, counts), unused = lax.scan(accumulate, start, (feats_blocks, dest_blocks))
    msg_total = jnp.dot(hidden_sum, w_msg_out.astype(jnp.float32), precision=lax.Precision.HIGHEST)
    aggregate = (msg_total / jnp.maximum(counts, 1.0)[:, None] + b_out).astype(jnp.bfloat16)
    gates_in = [jnp.dot(aggregate, w_input[g], preferred_element_type=jnp.float32) + b_input[g] for g in range(3)]
    gates_st = [jnp.dot(memory, w_hidden[g], preferred_element_type=jnp.float32) + b_hidden[g] for g in range(3)]
    reset_gate = jax.nn.sigmoid(gates_in[0] + gates_st[0])
    update_gate = jax.nn.sigmoid(gates_in[1] + gates_st[1])
    candidate = jnp.tanh(gates_in[2] + reset_gate * gates_st[2])
    old_state = memory.astype(jnp.float32)
    updated = (1.0 - update_gate) * candidate + update_gate * old_state
    new_memory = jnp.where((counts > 0.0)[:, None], updated, old_state).astype(jnp.bfloat16)

    block_of = (jnp.arange(QUERIES, dtype=jnp.int32) // Q_DEV).astype(jnp.int32)
    owner_of = (neighbours // STATE_CAP).astype(jnp.int32)
    place_of = (neighbours % STATE_CAP).astype(jnp.int32)
    node_of = owner_of * M_DEV + state_slots[owner_of * OWNERS + block_of[:, None], place_of]
    total = jnp.zeros((QUERIES, DM), jnp.float32)
    for k in range(NEIGH):
        total = total + new_memory[node_of[:, k]].astype(jnp.float32)
    neigh_mean = (total / NEIGH).astype(jnp.bfloat16)
    self_state = new_memory[block_of * M_DEV + query_slots]
    summed = jnp.dot(neigh_mean, w_neigh, preferred_element_type=jnp.float32) + jnp.dot(self_state, w_self, preferred_element_type=jnp.float32)
    embedding = jax.nn.relu(summed + b_embed).astype(jnp.bfloat16)
    return new_memory, embedding
```

```python
import functools

import jax
import jax.numpy as jnp
from jax import lax
from jax.experimental import pallas as pl
from jax.experimental.pallas import tpu as pltpu
from jax.sharding import PartitionSpec as P

BF = jnp.bfloat16
F32 = jnp.float32
MESH = pl.DeviceIdType.MESH
LANES = 128


def iota(shape, dim):
    return lax.broadcasted_iota(jnp.int32, shape, dim)


def fiota(shape, dim):
    return iota(shape, dim).astype(F32)


def ones_where(cond):
    return jnp.where(cond, 1.0, 0.0)


def to_col(row):
    size = row.shape[1]
    eye = iota((size, size), 0) == iota((size, size), 1)
    return jnp.sum(jnp.where(eye, row, 0.0), axis=1, keepdims=True)


def to_row(col):
    size = col.shape[0]
    eye = iota((size, size), 0) == iota((size, size), 1)
    return jnp.sum(jnp.where(eye, col, 0.0), axis=0, keepdims=True)


def dot(a, b):
    return jnp.dot(a, b, preferred_element_type=F32)


def kernel(
    n,
    owner_ref, slot_ref, b_msg_ref, b_out_ref, b_in_ref, b_hid_ref,
    sslots_ref, neigh_ref, query_ref, b_emb_ref,
    feats_hbm, mem_hbm, wev_hbm, wst_hbm, wout_hbm, win_hbm, whid_hbm, wn_hbm, ws_hbm,
    new_ref, emb_ref,
    feats, mem, wev, wst, wout, win, whid, wn, ws,
    target, slotcol, send_buf, ids_send, arr, ids, proj_hi, proj_lo, gst,
    acc, cnt, ar_s1, ar_r1, p_own, ar_s2, ar_r2, agg_own, agg_oth,
    smat, cmat, qmat, newm, st_send, st_recv, selfp, rs_send, rs_recv,
    load_sem, ds_sem, dr_sem, is_sem, ir_sem, xs_sem, xr_sem,
    c1s_sem, c1r_sem, c2s_sem, c2r_sem, ar_ssem, ar_rsem, ss_sem, sr_sem, rs_ssem, rs_rsem,
):
    me = lax.axis_index("nodes")
    m = lax.axis_index("mp")
    core = m + 1 - 2 * (m % 2)
    cross = (m + 2) % 4
    far = (core + 2) % 4
    events = owner_ref.shape[1]
    cap = send_buf.shape[1]
    nodes = mem.shape[0]
    width = mem.shape[1]
    share = width // 4
    half = width // 2
    scap = sslots_ref.shape[1]
    qblock = emb_ref.shape[0]
    fcols = feats.shape[1]

    loads = []

    def load(src, dst):
        c = pltpu.make_async_copy(src, dst, load_sem.at[len(loads)])
        c.start()
        loads.append(c)
        return c

    ld_feats = load(feats_hbm.at[:, pl.ds(pl.multiple_of(m * fcols, fcols), fcols)], feats)
    ld_mem = load(mem_hbm, mem)
    ld_wst = load(wst_hbm, wst)
    ld_wev = load(wev_hbm, wev)
    ld_whid = load(whid_hbm, whid)
    ld_wout = load(wout_hbm, wout)
    ld_win = load(win_hbm, win)
    ld_ws = load(ws_hbm, ws)
    ld_wn = load(wn_hbm, wn)

    barrier = pltpu.get_barrier_semaphore()

    def greet(k, c):
        pl.semaphore_signal(barrier, inc=1, device_id=((me + k) % n, m), device_id_type=MESH)
        return c

    lax.fori_loop(1, n, greet, 0)
    pl.semaphore_signal(barrier, inc=1, device_id=(me, core), device_id_type=MESH)
    pl.semaphore_signal(barrier, inc=1, device_id=(me, cross), device_id_type=MESH)

    rows = max(n, 16)
    oi = iota((rows, LANES), 0)
    tri = ones_where(iota((LANES, LANES), 0) < iota((LANES, LANES), 1)).astype(BF)
    running = jnp.zeros((rows, 1), F32)
    for j in range(events // LANES):
        at = slice(j * LANES, (j + 1) * LANES)
        ow = owner_ref[:, at]
        match = ones_where(ow == oi)
        before = dot(match.astype(BF), tri) + running
        place = jnp.sum(match * before, axis=0, keepdims=True)
        target[:, at] = ow.astype(F32) * float(cap) + place
        running = running + jnp.sum(match, axis=1, keepdims=True)
        col = to_col(slot_ref[:, at].astype(F32) + 1.0)
        slotcol[at, :] = jnp.broadcast_to(col, (LANES, LANES)).astype(BF)

    pl.semaphore_wait(barrier, n + 1)
    ld_feats.wait()

    def dispatch_copies(d, s):
        return (
            pltpu.make_async_remote_copy(
                src_ref=send_buf.at[d], dst_ref=arr.at[m, s],
                send_sem=ds_sem.at[d], recv_sem=dr_sem.at[s],
                device_id=(d, m), device_id_type=MESH,
            ),
            pltpu.make_async_remote_copy(
                src_ref=ids_send.at[d], dst_ref=ids.at[s],
                send_sem=is_sem.at[d], recv_sem=ir_sem.at[s],
                device_id=(d, m), device_id_type=MESH,
            ),
        )

    def dispatch(k, c):
        d = (me + k) % n
        pick = ones_where(
            target[...] == fiota((cap, events), 0) + (d * cap).astype(F32)
        ).astype(BF)
        out = dot(pick, jnp.concatenate([feats[...], slotcol[...]], axis=1))
        block = out[:, :fcols].astype(BF)
        idrow = jnp.broadcast_to(to_row(out[:, fcols:fcols + 1]), (8, cap))

        @pl.when(k < n)
        def _():
            send_buf[d] = block
            ids_send[d] = idrow
            for cp in dispatch_copies(d, me):
                cp.start()

        @pl.when(k == n)
        def _():
            arr[m, me] = block
            ids[me] = idrow

        return c

    lax.fori_loop(1, n + 1, dispatch, 0)

    ld_mem.wait()
    ld_wst.wait()
    proj = dot(mem[...], wst[...]) + b_msg_ref[...]
    hi = proj.astype(BF)
    proj_hi[...] = hi
    proj_lo[...] = (proj - hi.astype(F32)).astype(BF)
    acc[...] = jnp.zeros_like(acc)
    cnt[...] = jnp.zeros_like(cnt)
    ld_wev.wait()

    def relay(src_col, s, to, ssem, rsem):
        return pltpu.make_async_remote_copy(
            src_ref=arr.at[src_col, s], dst_ref=arr.at[src_col, s],
            send_sem=ssem.at[s], recv_sem=rsem.at[s],
            device_id=(me, to), device_id_type=MESH,
        )

    def step(i, c):
        @pl.when(i < n)
        def _():
            s = (me - i + n) % n

            @pl.when(i > 0)
            def _():
                for cp in dispatch_copies(s, s):
                    cp.wait_recv()

            relay(m, s, cross, xs_sem, xr_sem).start()
            relay(m, s, core, c1s_sem, c1r_sem).start()

        @pl.when(jnp.logical_and(i >= 1, i <= n))
        def _():
            s = (me - i + 1 + n) % n
            relay(cross, s, cross, xs_sem, xr_sem).wait_recv()
            relay(cross, s, core, c2s_sem, c2r_sem).start()

        @pl.when(i >= 2)
        def _():
            s = (me - i + 2 + n) % n
            relay(core, s, core, c1s_sem, c1r_sem).wait_recv()
            relay(far, s, core, c2s_sem, c2r_sem).wait_recv()
            x = jnp.concatenate([arr[j, s] for j in range(4)], axis=1)
            row = ids[s][0:1, :]
            oh = ones_where(to_col(row) == fiota((cap, nodes), 1) + 1.0).astype(BF)
            oht = ones_where(row == fiota((nodes, cap), 0) + 1.0)
            pre = dot(x, wev[...]) + dot(oh, proj_hi[...]) + dot(oh, proj_lo[...])
            hidden = jnp.maximum(pre, 0.0).astype(BF)
            acc[...] += dot(oht.astype(BF), hidden)
            cnt[...] += jnp.sum(oht, axis=1, keepdims=True)

        @pl.when(i == 0)
        def _():
            for g in range(3):
                gst[g] = dot(mem[...], whid[g]) + b_hid_ref[g:g + 1, :]

        @pl.when(i == 1)
        def _():
            lane = iota((qmat.shape[0], cmat.shape[1]), 1)
            total = jnp.zeros(cmat.shape, F32)
            for k in range(neigh_ref.shape[1]):
                total = total + ones_where(neigh_ref[:, k:k + 1] == lane)
            cmat[...] = total.astype(BF)
            qcol = to_col(query_ref[...].astype(F32))
            qmat[...] = ones_where(qcol == fiota(qmat.shape, 1)).astype(BF)

            def fill(d, c):
                col = to_col(sslots_ref[pl.ds(d, 1), :].astype(F32))
                smat[pl.ds(pl.multiple_of(d * scap, scap), scap), :] = ones_where(
                    col == fiota((scap, nodes), 1)
                ).astype(BF)
                return c

            lax.fori_loop(0, n, fill, 0)

        return c

    ld_whid.wait()
    lax.fori_loop(0, n + 2, step, 0)

    ld_wout.wait()
    chunks = 2
    crows = nodes // chunks
    my_half = pl.ds(pl.multiple_of((m % 2) * half, half), half)
    its_half = pl.ds(pl.multiple_of((core % 2) * half, half), half)

    def ar_copy(stage, r, src, dst, to):
        at = pl.ds(r * crows, crows)
        return pltpu.make_async_remote_copy(
            src_ref=src.at[at, :], dst_ref=dst.at[at, :],
            send_sem=ar_ssem.at[stage * chunks + r], recv_sem=ar_rsem.at[stage * chunks + r],
            device_id=(me, to), device_id_type=MESH,
        )

    def sum_out(r, cols):
        at = pl.ds(r * crows, crows)
        a = acc[at, :]
        head = a.astype(BF)
        tail = (a - head.astype(F32)).astype(BF)
        w = wout[:, cols]
        return dot(head, w) + dot(tail, w)

    stage1 = [ar_copy(0, r, ar_s1, ar_r1, core) for r in range(chunks)]
    stage2 = [ar_copy(1, r, ar_s2, ar_r2, cross) for r in range(chunks)]
    stage3 = [ar_copy(2, r, agg_own, agg_oth, core) for r in range(chunks)]
    for r in range(chunks):
        at = pl.ds(r * crows, crows)
        ar_s1[at, :] = sum_out(r, its_half).astype(BF)
        stage1[r].start()
    for r in range(chunks):
        at = pl.ds(r * crows, crows)
        own = sum_out(r, my_half)
        stage1[r].wait_recv()
        own = own + ar_r1[at, :].astype(F32)
        p_own[at, :] = own
        ar_s2[at, :] = own.astype(BF)
        stage2[r].start()
    ld_win.wait()
    for r in range(chunks):
        at = pl.ds(r * crows, crows)
        stage2[r].wait_recv()
        total = p_own[at, :] + ar_r2[at, :].astype(F32)
        agg = total / jnp.maximum(cnt[at, :][:, 0:1], 1.0) + b_out_ref[:, my_half]
        agg_own[at, :] = agg.astype(BF)
        stage3[r].start()
    for r in range(chunks):
        at = pl.ds(r * crows, crows)
        mine = [dot(agg_own[at, :], win[g, my_half, :]) for g in range(3)]
        stage3[r].wait_recv()
        gin = [
            mine[g] + dot(agg_oth[at, :], win[g, its_half, :]) + b_in_ref[g:g + 1, :]
            for g in range(3)
        ]
        reset = jax.nn.sigmoid(gin[0] + gst[0, at, :])
        update = jax.nn.sigmoid(gin[1] + gst[1, at, :])
        cand = jnp.tanh(gin[2] + reset * gst[2, at, :])
        old = mem[at, pl.ds(pl.multiple_of(m * share, share), share)].astype(F32)
        upd = (1.0 - update) * cand + update * old
        out = jnp.where(cnt[at, :][:, 0:1] > 0.0, upd, old).astype(BF)
        newm[at, :] = out
        new_ref[at, :] = out

    def state_copy(d, s):
        return pltpu.make_async_remote_copy(
            src_ref=st_send.at[pl.ds(pl.multiple_of(d * scap, scap), scap), :],
            dst_ref=st_recv.at[pl.ds(pl.multiple_of(s * scap, scap), scap), :],
            send_sem=ss_sem.at[d], recv_sem=sr_sem.at[s],
            device_id=(d, m), device_id_type=MESH,
        )

    st_send[...] = dot(smat[...], newm[...]).astype(BF)

    def send_state(k, c):
        state_copy((me + k) % n, me).start()
        return c

    lax.fori_loop(1, n, send_state, 0)
    mine = pl.ds(pl.multiple_of(me * scap, scap), scap)
    st_recv[mine, :] = st_send[mine, :]
    ld_ws.wait()
    selfp[...] = dot(dot(qmat[...], newm[...]).astype(BF), ws[...])
    ld_wn.wait()

    def recv_state(k, c):
        s = (me - k + n) % n
        state_copy(s, s).wait_recv()
        return c

    lax.fori_loop(1, n, recv_state, 0)

    def rs_copy(j, to):
        return pltpu.make_async_remote_copy(
            src_ref=rs_send.at[j], dst_ref=rs_recv.at[j],
            send_sem=rs_ssem.at[j], recv_sem=rs_rsem.at[j],
            device_id=(me, to), device_id_type=MESH,
        )

    def embed(b):
        at = pl.ds(pl.multiple_of(b * qblock, qblock), qblock)
        mean = (dot(cmat[at, :], st_recv[...]) / float(neigh_ref.shape[1])).astype(BF)
        return dot(mean, wn[...]) + selfp[at, :]

    to_core = [rs_copy(0, core), rs_copy(1, core)]
    to_cross = rs_copy(2, cross)
    rs_send[0] = embed(far).astype(BF)
    to_core[0].start()
    rs_send[1] = embed(core).astype(BF)
    to_core[1].start()
    part = embed(cross)
    to_core[0].wait_recv()
    rs_send[2] = (part + rs_recv[0].astype(F32)).astype(BF)
    to_cross.start()
    part = embed(m)
    to_core[1].wait_recv()
    part = part + rs_recv[1].astype(F32) + b_emb_ref[...]
    to_cross.wait_recv()
    emb_ref[...] = jnp.maximum(part + rs_recv[2].astype(F32), 0.0).astype(BF)

    def drain(s, c):
        relay(m, s, cross, xs_sem, xr_sem).wait_send()
        relay(m, s, core, c1s_sem, c1r_sem).wait_send()
        relay(cross, s, core, c2s_sem, c2r_sem).wait_send()
        return c

    lax.fori_loop(0, n, drain, 0)

    def drain_peers(k, c):
        d = (me + k) % n
        for cp in dispatch_copies(d, me):
            cp.wait_send()
        state_copy(d, me).wait_send()
        return c

    lax.fori_loop(1, n, drain_peers, 0)
    for cp in stage1 + stage2 + stage3 + to_core + [to_cross]:
        cp.wait_send()


def per_device(
    event_feats, event_owner, event_slot, memory, w_msg_event, w_msg_state, b_msg, w_msg_out,
    b_out, w_input, w_hidden, b_input, b_hidden, state_slots, neighbours, query_slots,
    w_neigh, w_self, b_embed,
):
    n = lax.axis_size("nodes")
    shares = lax.axis_size("mp")
    assert shares == 4
    events, feat = event_feats.shape
    nodes, width = memory.shape
    cap = 2 * events // n
    share = width // shares
    hid = w_msg_event.shape[1]
    half = width // 2
    scap = state_slots.shape[1]
    queries = query_slots.shape[0]
    qblock = queries // shares
    fcols = feat // shares
    vm = pl.BlockSpec(memory_space=pltpu.VMEM)
    hbm = pl.BlockSpec(memory_space=pl.ANY)
    V = pltpu.VMEM
    dma = lambda k: pltpu.SemaphoreType.DMA((k,))
    scratch = [
        V((events, fcols), BF), V(memory.shape, BF), V(w_msg_event.shape, BF),
        V(w_msg_state.shape, BF), V(w_msg_out.shape, BF), V(w_input.shape, BF),
        V(w_hidden.shape, BF), V(w_neigh.shape, BF), V(w_self.shape, BF),
        V((1, events), F32), V((events, LANES), BF), V((n, cap, fcols), BF),
        V((n, 8, cap), F32), V((4, n, cap, fcols), BF), V((n, 8, cap), F32),
        V((nodes, hid), BF), V((nodes, hid), BF), V((3, nodes, share), F32),
        V((nodes, hid), F32), V((nodes, LANES), F32),
        V((nodes, half), BF), V((nodes, half), BF), V((nodes, half), F32),
        V((nodes, half), BF), V((nodes, half), BF), V((nodes, half), BF), V((nodes, half), BF),
        V((n * scap, nodes), BF), V((queries, n * scap), BF), V((queries, nodes), BF),
        V((nodes, share), BF), V((n * scap, share), BF), V((n * scap, share), BF),
        V((queries, width), F32), V((3, qblock, width), BF), V((3, qblock, width), BF),
        dma(9), dma(n), dma(n), dma(n), dma(n), dma(n), dma(n),
        dma(n), dma(n), dma(n), dma(n), dma(6), dma(6), dma(n), dma(n), dma(3), dma(3),
    ]
    return pl.pallas_call(
        functools.partial(kernel, n),
        out_shape=(
            jax.ShapeDtypeStruct((nodes, share), BF),
            jax.ShapeDtypeStruct((qblock, width), BF),
        ),
        in_specs=[vm] * 10 + [hbm] * 9,
        out_specs=(vm, vm),
        scratch_shapes=scratch,
        compiler_params=pltpu.CompilerParams(
            collective_id=0, has_side_effects=True, vmem_limit_bytes=40 * 1024 * 1024
        ),
        cost_estimate=pl.CostEstimate(flops=8_000_000_000, bytes_accessed=9_000_000, transcendentals=0),
    )(
        event_owner.reshape(1, events), event_slot.reshape(1, events), b_msg.reshape(1, -1),
        b_out.reshape(1, -1), b_input, b_hidden, state_slots, neighbours,
        query_slots.reshape(1, -1), b_embed.reshape(1, -1),
        event_feats, memory, w_msg_event, w_msg_state, w_msg_out, w_input, w_hidden,
        w_neigh, w_self,
    )


def solution(mesh):
    in_specs = (
        P("nodes", None),
        P("nodes", None),
        P("nodes"),
        P("nodes", None),
        P(None, "mp"),
        P(None, "mp"),
        P("mp"),
        P("mp", None),
        P(),
        P(None, None, "mp"),
        P(None, None, "mp"),
        P(None, "mp"),
        P(None, "mp"),
        P("nodes", None),
        P("nodes", None),
        P("nodes"),
        P("mp", None),
        P("mp", None),
        P(),
    )
    out_specs = (P("nodes", "mp"), P(("nodes", "mp"), None))
    return jax.shard_map(
        per_device, mesh=mesh, in_specs=in_specs, out_specs=out_specs, check_vma=False
    )
```

```python
import functools

import jax
import jax.numpy as jnp
from jax import lax
from jax.experimental import pallas as pl
from jax.experimental.pallas import tpu as pltpu
from jax.sharding import PartitionSpec as P

BF = jnp.bfloat16
F32 = jnp.float32
MESH = pl.DeviceIdType.MESH
LANES = 128
AR_CHUNKS = 4


def iota(shape, dim):
    return lax.broadcasted_iota(jnp.int32, shape, dim)


def fiota(shape, dim):
    return iota(shape, dim).astype(F32)


def ones_where(cond):
    return jnp.where(cond, 1.0, 0.0)


def to_col(row):
    size = row.shape[1]
    eye = iota((size, size), 0) == iota((size, size), 1)
    return jnp.sum(jnp.where(eye, row, 0.0), axis=1, keepdims=True)


def to_row(col):
    size = col.shape[0]
    eye = iota((size, size), 0) == iota((size, size), 1)
    return jnp.sum(jnp.where(eye, col, 0.0), axis=0, keepdims=True)


def dot(a, b):
    return jnp.dot(a, b, preferred_element_type=F32)


def kernel(
    n,
    owner_hbm, slot_hbm, b_msg_hbm, b_out_hbm, b_in_hbm, b_hid_hbm,
    sslots_hbm, neigh_hbm, query_hbm, b_emb_hbm,
    feats_hbm, mem_hbm, wev_hbm, wst_hbm, wout_hbm, win_hbm, whid_hbm, wn_hbm, ws_hbm,
    new_ref, emb_ref,
    owner_ref, slot_ref, b_msg_ref, b_out_ref, b_in_ref, b_hid_ref,
    sslots_ref, neigh_ref, query_ref, b_emb_ref,
    feats, mem, wev, wst, wout, win, whid, wn, ws,
    target, slotcol, send_buf, ids_send, arr, ids, proj_ref, gst,
    acc, cnt, ar_s1, ar_r1, p_own, ar_s2, ar_r2, agg_own, agg_oth,
    smat, cmat, qmat, newm, st_send, st_recv, selfp, rs_send, rs_recv,
    load_sem, ds_sem, dr_sem, is_sem, ir_sem, xs_sem, xr_sem,
    c1s_sem, c1r_sem, c2s_sem, c2r_sem, ar_ssem, ar_rsem, ss_sem, sr_sem, rs_ssem, rs_rsem,
):
    me = lax.axis_index("nodes")
    m = lax.axis_index("mp")
    core = m + 1 - 2 * (m % 2)
    cross = (m + 2) % 4
    far = (core + 2) % 4
    events = owner_hbm.shape[1]
    cap = send_buf.shape[1]
    nodes = mem.shape[0]
    width = mem.shape[1]
    share = width // 4
    half = width // 2
    scap = sslots_ref.shape[1]
    qblock = emb_ref.shape[0]
    fcols = feats.shape[1]

    loads = []

    def load(src, dst):
        c = pltpu.make_async_copy(src, dst, load_sem.at[len(loads)])
        c.start()
        loads.append(c)
        return c

    ld_owner = load(owner_hbm, owner_ref)
    ld_slot = load(slot_hbm, slot_ref)
    ld_feats = load(feats_hbm.at[:, pl.ds(pl.multiple_of(m * fcols, fcols), fcols)], feats)
    ld_mem = load(mem_hbm, mem)
    ld_wst = load(wst_hbm, wst)
    ld_b_msg = load(b_msg_hbm, b_msg_ref)
    ld_wev = load(wev_hbm, wev)
    ld_whid = load(whid_hbm, whid)
    ld_small = [
        load(b_hid_hbm, b_hid_ref), load(sslots_hbm, sslots_ref), load(neigh_hbm, neigh_ref),
        load(query_hbm, query_ref), load(b_out_hbm, b_out_ref), load(b_in_hbm, b_in_ref),
        load(b_emb_hbm, b_emb_ref),
    ]
    ld_wout = load(wout_hbm, wout)
    ld_win = load(win_hbm, win)
    ld_ws = load(ws_hbm, ws)
    ld_wn = load(wn_hbm, wn)

    barrier = pltpu.get_barrier_semaphore()

    def greet(k, c):
        pl.semaphore_signal(barrier, inc=1, device_id=((me + k) % n, m), device_id_type=MESH)
        return c

    lax.fori_loop(1, n, greet, 0)
    pl.semaphore_signal(barrier, inc=1, device_id=(me, core), device_id_type=MESH)
    pl.semaphore_signal(barrier, inc=1, device_id=(me, cross), device_id_type=MESH)

    ld_owner.wait()
    ld_slot.wait()
    rows = max(n, 16)
    oi = iota((rows, LANES), 0)
    tri = ones_where(iota((LANES, LANES), 0) < iota((LANES, LANES), 1)).astype(BF)
    running = jnp.zeros((rows, 1), F32)
    for j in range(events // LANES):
        at = slice(j * LANES, (j + 1) * LANES)
        ow = owner_ref[:, at]
        match = ones_where(ow == oi)
        before = dot(match.astype(BF), tri) + running
        place = jnp.sum(match * before, axis=0, keepdims=True)
        target[:, at] = ow.astype(F32) * float(cap) + place
        running = running + jnp.sum(match, axis=1, keepdims=True)
        col = to_col(slot_ref[:, at].astype(F32) + 1.0)
        slotcol[at, :] = jnp.broadcast_to(col, (LANES, LANES)).astype(BF)

    pl.semaphore_wait(barrier, n + 1)
    ld_feats.wait()

    def dispatch_copies(d, s):
        return (
            pltpu.make_async_remote_copy(
                src_ref=send_buf.at[d], dst_ref=arr.at[m, s],
                send_sem=ds_sem.at[d], recv_sem=dr_sem.at[s],
                device_id=(d, m), device_id_type=MESH,
            ),
            pltpu.make_async_remote_copy(
                src_ref=ids_send.at[d], dst_ref=ids.at[s],
                send_sem=is_sem.at[d], recv_sem=ir_sem.at[s],
                device_id=(d, m), device_id_type=MESH,
            ),
        )

    def relay(src_col, s, to, ssem, rsem):
        return pltpu.make_async_remote_copy(
            src_ref=arr.at[src_col, s], dst_ref=arr.at[src_col, s],
            send_sem=ssem.at[s], recv_sem=rsem.at[s],
            device_id=(me, to), device_id_type=MESH,
        )

    mid = n // 2
    here, place_in = me // mid, me % mid
    there = (here + 1) % 2

    def source(u):
        far_side = u // mid
        return ((here + far_side) % 2) * mid + (place_in - u % mid + mid) % mid

    def block_for(d):
        pick = ones_where(
            target[...] == fiota((cap, events), 0) + (d * cap).astype(F32)
        ).astype(BF)
        out = dot(pick, jnp.concatenate([feats[...], slotcol[...]], axis=1))
        idrow = jnp.broadcast_to(to_row(out[:, fcols:fcols + 1]), (8, cap))
        return out[:, :fcols].astype(BF), idrow

    def pass_on(u):
        s = source(u)
        relay(m, s, cross, xs_sem, xr_sem).start()
        relay(m, s, core, c1s_sem, c1r_sem).start()

    def arrive(u):
        s = source(u)
        for cp in dispatch_copies(s, s):
            cp.wait_recv()
        pass_on(u)

    def forward(u):
        s = source(u)
        relay(cross, s, cross, xs_sem, xr_sem).wait_recv()
        relay(cross, s, core, c2s_sem, c2r_sem).start()

    def absorb(u):
        s = source(u)
        relay(core, s, core, c1s_sem, c1r_sem).wait_recv()
        relay(far, s, core, c2s_sem, c2r_sem).wait_recv()
        x = jnp.concatenate([arr[j, s] for j in range(4)], axis=1)
        row = ids[s][0:1, :]
        oh = ones_where(to_col(row) == fiota((cap, nodes), 1) + 1.0).astype(BF)
        oht = ones_where(row == fiota((nodes, cap), 0) + 1.0)
        pre = dot(x, wev[...]) + dot(oh, proj_ref[...])
        hidden = jnp.maximum(pre, 0.0).astype(BF)
        acc[...] += dot(oht.astype(BF), hidden)
        cnt[...] += jnp.sum(oht, axis=1, keepdims=True)

    block, idrow = block_for(me)
    arr[m, me] = block
    ids[me] = idrow
    pass_on(0)

    def dispatch(t, c):
        across = t % 2
        d = ((here + across) % 2) * mid + (place_in + t // 2) % mid
        block, idrow = block_for(d)
        send_buf[d] = block
        ids_send[d] = idrow
        for cp in dispatch_copies(d, me):
            cp.start()

        @pl.when(jnp.logical_and(t >= 4, t % 2 == 0))
        def _():
            arrive(t // 2 - 1)

        return c

    lax.fori_loop(1, n, dispatch, 0)

    acc[...] = jnp.zeros_like(acc)
    cnt[...] = jnp.zeros_like(cnt)
    ld_mem.wait()
    ld_wst.wait()
    ld_b_msg.wait()
    proj_ref[...] = (dot(mem[...], wst[...]) + b_msg_ref[...]).astype(BF)
    ld_wev.wait()
    ld_whid.wait()
    for ld in ld_small:
        ld.wait()

    def each(body):
        def run(u, c):
            body(u)
            return c

        return run

    lax.fori_loop(0, mid - 3, each(forward), 0)
    lax.fori_loop(0, mid - 4, each(absorb), 0)

    def step(i, c):
        @pl.when(i < n)
        def _():
            arrive(i)

        @pl.when(i < n + 2)
        def _():
            forward(i - 2)

        @pl.when(i == mid + 1)
        def _():
            for g in range(3):
                gst[g] = dot(mem[...], whid[g]) + b_hid_ref[g:g + 1, :]

        @pl.when(i == mid + 2)
        def _():
            place = iota((cmat.shape[1], cmat.shape[0]), 0)
            total = jnp.zeros((cmat.shape[1], cmat.shape[0]), F32)
            for k in range(neigh_ref.shape[0]):
                total = total + ones_where(neigh_ref[k:k + 1, :] == place)
            cmat[...] = total.T.astype(BF)
            qcol = to_col(query_ref[...].astype(F32))
            qmat[...] = ones_where(qcol == fiota(qmat.shape, 1)).astype(BF)

            def fill(d, c):
                col = to_col(sslots_ref[pl.ds(d, 1), :].astype(F32))
                smat[pl.ds(pl.multiple_of(d * scap, scap), scap), :] = ones_where(
                    col == fiota((scap, nodes), 1)
                ).astype(BF)
                return c

            lax.fori_loop(0, n, fill, 0)

        absorb(i - 3)
        return c

    lax.fori_loop(mid - 1, n + 3, step, 0)

    ld_wout.wait()
    chunks = AR_CHUNKS
    crows = nodes // chunks
    my_half = pl.ds(pl.multiple_of((m % 2) * half, half), half)
    its_half = pl.ds(pl.multiple_of((core % 2) * half, half), half)

    def ar_copy(stage, r, src, dst, to):
        at = pl.ds(r * crows, crows)
        return pltpu.make_async_remote_copy(
            src_ref=src.at[at, :], dst_ref=dst.at[at, :],
            send_sem=ar_ssem.at[stage * chunks + r], recv_sem=ar_rsem.at[stage * chunks + r],
            device_id=(me, to), device_id_type=MESH,
        )

    def sum_out(r, cols):
        at = pl.ds(r * crows, crows)
        return dot(acc[at, :].astype(BF), wout[:, cols])

    stage1 = [ar_copy(0, r, ar_s1, ar_r1, core) for r in range(chunks)]
    stage2 = [ar_copy(1, r, ar_s2, ar_r2, cross) for r in range(chunks)]
    stage3 = [ar_copy(2, r, agg_own, agg_oth, core) for r in range(chunks)]
    for r in range(chunks):
        at = pl.ds(r * crows, crows)
        ar_s1[at, :] = sum_out(r, its_half).astype(BF)
        stage1[r].start()
    for r in range(chunks):
        at = pl.ds(r * crows, crows)
        own = sum_out(r, my_half)
        stage1[r].wait_recv()
        own = own + ar_r1[at, :].astype(F32)
        p_own[at, :] = own
        ar_s2[at, :] = own.astype(BF)
        stage2[r].start()
    ld_win.wait()
    for r in range(chunks):
        at = pl.ds(r * crows, crows)
        stage2[r].wait_recv()
        total = p_own[at, :] + ar_r2[at, :].astype(F32)
        agg = total / jnp.maximum(cnt[at, :][:, 0:1], 1.0) + b_out_ref[:, my_half]
        agg_own[at, :] = agg.astype(BF)
        stage3[r].start()
    for r in range(chunks):
        at = pl.ds(r * crows, crows)
        mine = [dot(agg_own[at, :], win[g, my_half, :]) for g in range(3)]
        stage3[r].wait_recv()
        gin = [
            mine[g] + dot(agg_oth[at, :], win[g, its_half, :]) + b_in_ref[g:g + 1, :]
            for g in range(3)
        ]
        reset = jax.nn.sigmoid(gin[0] + gst[0, at, :])
        update = jax.nn.sigmoid(gin[1] + gst[1, at, :])
        cand = jnp.tanh(gin[2] + reset * gst[2, at, :])
        old = mem[at, pl.ds(pl.multiple_of(m * share, share), share)].astype(F32)
        upd = (1.0 - update) * cand + update * old
        out = jnp.where(cnt[at, :][:, 0:1] > 0.0, upd, old).astype(BF)
        newm[at, :] = out
        new_ref[at, :] = out

    def state_copy(d, s):
        return pltpu.make_async_remote_copy(
            src_ref=st_send.at[pl.ds(pl.multiple_of(d * scap, scap), scap), :],
            dst_ref=st_recv.at[pl.ds(pl.multiple_of(s * scap, scap), scap), :],
            send_sem=ss_sem.at[d], recv_sem=sr_sem.at[s],
            device_id=(d, m), device_id_type=MESH,
        )

    st_send[...] = dot(smat[...], newm[...]).astype(BF)

    def send_state(k, c):
        state_copy((me + k) % n, me).start()
        return c

    lax.fori_loop(1, n, send_state, 0)
    mine = pl.ds(pl.multiple_of(me * scap, scap), scap)
    st_recv[mine, :] = st_send[mine, :]
    ld_ws.wait()
    selfp[...] = dot(dot(qmat[...], newm[...]).astype(BF), ws[...])
    ld_wn.wait()

    def recv_state(k, c):
        s = (me - k + n) % n
        state_copy(s, s).wait_recv()
        return c

    lax.fori_loop(1, n, recv_state, 0)

    def rs_copy(j, to):
        return pltpu.make_async_remote_copy(
            src_ref=rs_send.at[j], dst_ref=rs_recv.at[j],
            send_sem=rs_ssem.at[j], recv_sem=rs_rsem.at[j],
            device_id=(me, to), device_id_type=MESH,
        )

    def embed(b):
        at = pl.ds(pl.multiple_of(b * qblock, qblock), qblock)
        mean = (dot(cmat[at, :], st_recv[...]) / float(neigh_ref.shape[0])).astype(BF)
        return dot(mean, wn[...]) + selfp[at, :]

    to_core = [rs_copy(0, core), rs_copy(1, core)]
    to_cross = rs_copy(2, cross)
    rs_send[0] = embed(far).astype(BF)
    to_core[0].start()
    rs_send[1] = embed(core).astype(BF)
    to_core[1].start()
    part = embed(cross)
    to_core[0].wait_recv()
    rs_send[2] = (part + rs_recv[0].astype(F32)).astype(BF)
    to_cross.start()
    part = embed(m)
    to_core[1].wait_recv()
    part = part + rs_recv[1].astype(F32) + b_emb_ref[...]
    to_cross.wait_recv()
    emb_ref[...] = jnp.maximum(part + rs_recv[2].astype(F32), 0.0).astype(BF)

    def drain(s, c):
        relay(m, s, cross, xs_sem, xr_sem).wait_send()
        relay(m, s, core, c1s_sem, c1r_sem).wait_send()
        relay(cross, s, core, c2s_sem, c2r_sem).wait_send()
        return c

    lax.fori_loop(0, n, drain, 0)

    def drain_peers(k, c):
        d = (me + k) % n
        for cp in dispatch_copies(d, me):
            cp.wait_send()
        state_copy(d, me).wait_send()
        return c

    lax.fori_loop(1, n, drain_peers, 0)
    for cp in stage1 + stage2 + stage3 + to_core + [to_cross]:
        cp.wait_send()


def per_device(
    event_feats, event_owner, event_slot, memory, w_msg_event, w_msg_state, b_msg, w_msg_out,
    b_out, w_input, w_hidden, b_input, b_hidden, state_slots, neighbours, query_slots,
    w_neigh, w_self, b_embed,
):
    n = lax.axis_size("nodes")
    shares = lax.axis_size("mp")
    assert shares == 4
    events, feat = event_feats.shape
    nodes, width = memory.shape
    cap = 2 * events // n
    share = width // shares
    hid = w_msg_event.shape[1]
    half = width // 2
    scap = state_slots.shape[1]
    queries = query_slots.shape[0]
    qblock = queries // shares
    fcols = feat // shares
    vm = pl.BlockSpec(memory_space=pltpu.VMEM)
    hbm = pl.BlockSpec(memory_space=pl.ANY)
    V = pltpu.VMEM
    dma = lambda k: pltpu.SemaphoreType.DMA((k,))
    scratch = [
        V((1, events), jnp.int32), V((1, events), jnp.int32), V((1, hid), F32),
        V((1, width), F32), V(b_input.shape, F32), V(b_hidden.shape, F32),
        V(state_slots.shape, jnp.int32), V(neighbours.shape[::-1], jnp.int32),
        V((1, queries), jnp.int32), V((1, width), F32),
        V((events, fcols), BF), V(memory.shape, BF), V(w_msg_event.shape, BF),
        V(w_msg_state.shape, BF), V(w_msg_out.shape, BF), V(w_input.shape, BF),
        V(w_hidden.shape, BF), V(w_neigh.shape, BF), V(w_self.shape, BF),
        V((1, events), F32), V((events, LANES), BF), V((n, cap, fcols), BF),
        V((n, 8, cap), F32), V((4, n, cap, fcols), BF), V((n, 8, cap), F32),
        V((nodes, hid), BF), V((3, nodes, share), F32),
        V((nodes, hid), F32), V((nodes, LANES), F32),
        V((nodes, half), BF), V((nodes, half), BF), V((nodes, half), F32),
        V((nodes, half), BF), V((nodes, half), BF), V((nodes, half), BF), V((nodes, half), BF),
        V((n * scap, nodes), BF), V((queries, n * scap), BF), V((queries, nodes), BF),
        V((nodes, share), BF), V((n * scap, share), BF), V((n * scap, share), BF),
        V((queries, width), F32), V((3, qblock, width), BF), V((3, qblock, width), BF),
        dma(19), dma(n), dma(n), dma(n), dma(n), dma(n), dma(n),
        dma(n), dma(n), dma(n), dma(n), dma(3 * AR_CHUNKS), dma(3 * AR_CHUNKS), dma(n), dma(n), dma(3), dma(3),
    ]
    return pl.pallas_call(
        functools.partial(kernel, n),
        out_shape=(
            jax.ShapeDtypeStruct((nodes, share), BF),
            jax.ShapeDtypeStruct((qblock, width), BF),
        ),
        in_specs=[hbm] * 19,
        out_specs=(vm, vm),
        scratch_shapes=scratch,
        compiler_params=pltpu.CompilerParams(
            collective_id=0, has_side_effects=True, vmem_limit_bytes=60 * 1024 * 1024
        ),
        cost_estimate=pl.CostEstimate(flops=8_000_000_000, bytes_accessed=9_000_000, transcendentals=0),
    )(
        event_owner.reshape(1, events), event_slot.reshape(1, events), b_msg.reshape(1, -1),
        b_out.reshape(1, -1), b_input, b_hidden, state_slots, neighbours.T,
        query_slots.reshape(1, -1), b_embed.reshape(1, -1),
        event_feats, memory, w_msg_event, w_msg_state, w_msg_out, w_input, w_hidden,
        w_neigh, w_self,
    )


def solution(mesh):
    in_specs = (
        P("nodes", None),
        P("nodes", None),
        P("nodes"),
        P("nodes", None),
        P(None, "mp"),
        P(None, "mp"),
        P("mp"),
        P("mp", None),
        P(),
        P(None, None, "mp"),
        P(None, None, "mp"),
        P(None, "mp"),
        P(None, "mp"),
        P("nodes", None),
        P("nodes", None),
        P("nodes"),
        P("mp", None),
        P("mp", None),
        P(),
    )
    out_specs = (P("nodes", "mp"), P(("nodes", "mp"), None))
    return jax.shard_map(
        per_device, mesh=mesh, in_specs=in_specs, out_specs=out_specs, check_vma=False
    )
```

```python
import functools

import jax
import jax.numpy as jnp
from jax import lax
from jax.experimental import pallas as pl
from jax.experimental.pallas import tpu as pltpu
from jax.sharding import PartitionSpec as P

BF = jnp.bfloat16
F32 = jnp.float32
MESH = pl.DeviceIdType.MESH
LANES = 128
AR_CHUNKS = 4
VMEM_BYTES = 60 * 1024 * 1024


def iota(shape, dim):
    return lax.broadcasted_iota(jnp.int32, shape, dim)


def fiota(shape, dim):
    return iota(shape, dim).astype(F32)


def ones_where(cond):
    return jnp.where(cond, 1.0, 0.0)


def to_col(row):
    size = row.shape[1]
    eye = iota((size, size), 0) == iota((size, size), 1)
    return jnp.sum(jnp.where(eye, row, 0.0), axis=1, keepdims=True)


def to_row(col):
    size = col.shape[0]
    eye = iota((size, size), 0) == iota((size, size), 1)
    return jnp.sum(jnp.where(eye, col, 0.0), axis=0, keepdims=True)


def dot(a, b):
    return jnp.dot(a, b, preferred_element_type=F32)


def kernel(
    n,
    owner_hbm, slot_hbm, b_msg_hbm, b_out_hbm, b_in_hbm, b_hid_hbm,
    sslots_hbm, neigh_hbm, query_hbm, b_emb_hbm,
    feats_hbm, mem_hbm, wev_hbm, wst_hbm, wout_hbm, win_hbm, whid_hbm, wn_hbm, ws_hbm,
    new_ref, emb_ref,
    owner_ref, slot_ref, b_msg_ref, b_out_ref, b_in_ref, b_hid_ref,
    sslots_ref, neigh_ref, query_ref, b_emb_ref,
    feats, mem, wev, wst, wout, win, whid, wn, ws,
    target, slotcol, send_buf, ids_send, arr, ids, proj_ref, gst,
    acc, cnt, ar_s1, ar_r1, p_own, ar_s2, ar_r2, agg_own, agg_oth,
    smat, cmat, qmat, newm, st_send, st_recv, selfp, rs_send, rs_recv,
    load_sem, ds_sem, dr_sem, is_sem, ir_sem, xs_sem, xr_sem,
    c1s_sem, c1r_sem, c2s_sem, c2r_sem, ar_ssem, ar_rsem, ss_sem, sr_sem, rs_ssem, rs_rsem,
):
    me = lax.axis_index("nodes")
    m = lax.axis_index("mp")
    core = m + 1 - 2 * (m % 2)
    cross = (m + 2) % 4
    far = (core + 2) % 4
    events = owner_hbm.shape[1]
    cap = send_buf.shape[1]
    nodes = mem.shape[0]
    width = mem.shape[1]
    share = width // 4
    half = width // 2
    scap = sslots_ref.shape[1]
    qblock = emb_ref.shape[0]
    fcols = feats.shape[1]

    loads = []

    def load(src, dst):
        c = pltpu.make_async_copy(src, dst, load_sem.at[len(loads)])
        c.start()
        loads.append(c)
        return c

    ld_owner = load(owner_hbm, owner_ref)
    ld_slot = load(slot_hbm, slot_ref)
    ld_feats = load(feats_hbm.at[:, pl.ds(pl.multiple_of(m * fcols, fcols), fcols)], feats)

    barrier = pltpu.get_barrier_semaphore()

    def greet(k, c):
        pl.semaphore_signal(barrier, inc=1, device_id=((me + k) % n, m), device_id_type=MESH)
        return c

    lax.fori_loop(1, n, greet, 0)
    pl.semaphore_signal(barrier, inc=1, device_id=(me, core), device_id_type=MESH)
    pl.semaphore_signal(barrier, inc=1, device_id=(me, cross), device_id_type=MESH)

    ld_owner.wait()
    ld_slot.wait()
    ld_mem = load(mem_hbm, mem)
    ld_wst = load(wst_hbm, wst)
    ld_b_msg = load(b_msg_hbm, b_msg_ref)
    ld_wev = load(wev_hbm, wev)
    ld_wout = load(wout_hbm, wout)
    ld_whid = load(whid_hbm, whid)
    ld_win = load(win_hbm, win)
    ld_small = [
        load(b_hid_hbm, b_hid_ref), load(sslots_hbm, sslots_ref), load(neigh_hbm, neigh_ref),
        load(query_hbm, query_ref), load(b_out_hbm, b_out_ref), load(b_in_hbm, b_in_ref),
        load(b_emb_hbm, b_emb_ref),
    ]
    ld_ws = load(ws_hbm, ws)
    ld_wn = load(wn_hbm, wn)
    rows = max(n, 16)
    oi = iota((rows, LANES), 0)
    tri = ones_where(iota((LANES, LANES), 0) < iota((LANES, LANES), 1)).astype(BF)
    running = jnp.zeros((rows, 1), F32)
    for j in range(events // LANES):
        at = slice(j * LANES, (j + 1) * LANES)
        ow = owner_ref[:, at]
        match = ones_where(ow == oi)
        before = dot(match.astype(BF), tri) + running
        place = jnp.sum(match * before, axis=0, keepdims=True)
        target[:, at] = ow.astype(F32) * float(cap) + place
        running = running + jnp.sum(match, axis=1, keepdims=True)
        col = to_col(slot_ref[:, at].astype(F32) + 1.0)
        slotcol[at, :] = jnp.broadcast_to(col, (LANES, LANES)).astype(BF)

    pl.semaphore_wait(barrier, n + 1)
    ld_feats.wait()

    def dispatch_copies(d, s):
        return (
            pltpu.make_async_remote_copy(
                src_ref=send_buf.at[d], dst_ref=arr.at[m, s],
                send_sem=ds_sem.at[d], recv_sem=dr_sem.at[s],
                device_id=(d, m), device_id_type=MESH,
            ),
            pltpu.make_async_remote_copy(
                src_ref=ids_send.at[d], dst_ref=ids.at[s],
                send_sem=is_sem.at[d], recv_sem=ir_sem.at[s],
                device_id=(d, m), device_id_type=MESH,
            ),
        )

    def relay(src_col, s, to, ssem, rsem):
        return pltpu.make_async_remote_copy(
            src_ref=arr.at[src_col, s], dst_ref=arr.at[src_col, s],
            send_sem=ssem.at[s], recv_sem=rsem.at[s],
            device_id=(me, to), device_id_type=MESH,
        )

    mid = n // 2
    here, place_in = me // mid, me % mid
    there = (here + 1) % 2

    def source(u):
        far_side = u // mid
        return ((here + far_side) % 2) * mid + (place_in - u % mid + mid) % mid

    def block_for(d):
        pick = ones_where(
            target[...] == fiota((cap, events), 0) + (d * cap).astype(F32)
        ).astype(BF)
        out = dot(pick, jnp.concatenate([feats[...], slotcol[...]], axis=1))
        return out[:, :fcols].astype(BF), to_row(out[:, fcols:fcols + 1])

    def pass_on(u):
        s = source(u)
        relay(m, s, cross, xs_sem, xr_sem).start()
        relay(m, s, core, c1s_sem, c1r_sem).start()

    def arrive(u):
        s = source(u)
        for cp in dispatch_copies(s, s):
            cp.wait_recv()
        pass_on(u)

    def forward(u):
        s = source(u)
        relay(cross, s, cross, xs_sem, xr_sem).wait_recv()
        relay(cross, s, core, c2s_sem, c2r_sem).start()

    def absorb(u):
        s = source(u)
        relay(core, s, core, c1s_sem, c1r_sem).wait_recv()
        relay(far, s, core, c2s_sem, c2r_sem).wait_recv()
        x = jnp.concatenate([arr[j, s] for j in range(4)], axis=1)
        row = ids[s]
        oh = ones_where(to_col(row) == fiota((cap, nodes), 1) + 1.0).astype(BF)
        oht = ones_where(row == fiota((nodes, cap), 0) + 1.0)
        pre = dot(x, wev[...]) + dot(oh, proj_ref[...])
        hidden = jnp.maximum(pre, 0.0).astype(BF)
        acc[...] += dot(oht.astype(BF), hidden)
        for lo in range(0, cap, LANES):
            wide = min(cap, LANES)
            cnt[:, 0:wide] += oht[:, lo:lo + wide]

    def send_block(t):
        d = ((here + (t + 1) % 2) % 2) * mid + (place_in + t // 2) % mid
        block, idrow = block_for(d)
        send_buf[d] = block
        ids_send[d] = idrow
        for cp in dispatch_copies(d, me):
            cp.start()

    send_block(0)
    block, idrow = block_for(me)
    arr[m, me] = block
    ids[me] = idrow
    pass_on(0)

    def dispatch(t, c):
        send_block(t)

        @pl.when(jnp.logical_and(t >= 5, t % 2 == 1))
        def _():
            arrive((t - 3) // 2)

        return c

    lax.fori_loop(2, n, dispatch, 0)

    acc[...] = jnp.zeros_like(acc)
    cnt[...] = jnp.zeros_like(cnt)
    ld_mem.wait()
    ld_wst.wait()
    ld_b_msg.wait()
    proj_ref[...] = (dot(mem[...], wst[...]) + b_msg_ref[...]).astype(BF)
    ld_wev.wait()
    def each(body):
        def run(u, c):
            body(u)
            return c

        return run

    lax.fori_loop(0, mid - 2, each(forward), 0)
    lax.fori_loop(0, mid - 3, each(absorb), 0)

    def step(i):
        arrive(i)
        forward(i - 1)
        absorb(i - 2)

    lax.fori_loop(mid - 1, n, each(step), 0)
    absorb(n - 2)
    forward(n - 1)
    absorb(n - 1)

    ld_wout.wait()
    chunks = AR_CHUNKS
    crows = nodes // chunks
    my_half = pl.ds(pl.multiple_of((m % 2) * half, half), half)
    its_half = pl.ds(pl.multiple_of((core % 2) * half, half), half)

    def ar_copy(stage, r, src, dst, to):
        at = pl.ds(r * crows, crows)
        return pltpu.make_async_remote_copy(
            src_ref=src.at[at, :], dst_ref=dst.at[at, :],
            send_sem=ar_ssem.at[stage * chunks + r], recv_sem=ar_rsem.at[stage * chunks + r],
            device_id=(me, to), device_id_type=MESH,
        )

    def sum_out(r, cols):
        at = pl.ds(r * crows, crows)
        return dot(acc[at, :].astype(BF), wout[:, cols])

    stage1 = [ar_copy(0, r, ar_s1, ar_r1, core) for r in range(chunks)]
    stage2 = [ar_copy(1, r, ar_s2, ar_r2, cross) for r in range(chunks)]
    stage3 = [ar_copy(2, r, agg_own, agg_oth, core) for r in range(chunks)]
    for r in range(chunks):
        at = pl.ds(r * crows, crows)
        ar_s1[at, :] = sum_out(r, its_half).astype(BF)
        stage1[r].start()
    for r in range(chunks):
        at = pl.ds(r * crows, crows)
        own = sum_out(r, my_half)
        stage1[r].wait_recv()
        own = own + ar_r1[at, :].astype(F32)
        p_own[at, :] = own
        ar_s2[at, :] = own.astype(BF)
        stage2[r].start()

    ld_whid.wait()
    for ld in ld_small:
        ld.wait()
    for g in range(3):
        gst[g] = dot(mem[...], whid[g]) + b_hid_ref[g:g + 1, :]
    cnt[...] = jnp.broadcast_to(jnp.sum(cnt[...], axis=1, keepdims=True), cnt.shape)

    def tables():
        place = iota((cmat.shape[1], cmat.shape[0]), 0)
        total = jnp.zeros((cmat.shape[1], cmat.shape[0]), F32)
        for k in range(neigh_ref.shape[0]):
            total = total + ones_where(neigh_ref[k:k + 1, :] == place)
        cmat[...] = total.T.astype(BF)
        qcol = to_col(query_ref[...].astype(F32))
        qmat[...] = ones_where(qcol == fiota(qmat.shape, 1)).astype(BF)

        def fill(d, c):
            col = to_col(sslots_ref[pl.ds(d, 1), :].astype(F32))
            smat[pl.ds(pl.multiple_of(d * scap, scap), scap), :] = ones_where(
                col == fiota((scap, nodes), 1)
            ).astype(BF)
            return c

        lax.fori_loop(0, n, fill, 0)

    def aggregate(r):
        at = pl.ds(r * crows, crows)
        stage2[r].wait_recv()
        total = p_own[at, :] + ar_r2[at, :].astype(F32)
        agg = total / jnp.maximum(cnt[at, :][:, 0:1], 1.0) + b_out_ref[:, my_half]
        agg_own[at, :] = agg.astype(BF)
        stage3[r].start()

    def gates(r):
        at = pl.ds(r * crows, crows)
        mine = [dot(agg_own[at, :], win[g, my_half, :]) for g in range(3)]
        stage3[r].wait_recv()
        gin = [
            mine[g] + dot(agg_oth[at, :], win[g, its_half, :]) + b_in_ref[g:g + 1, :]
            for g in range(3)
        ]
        reset = jax.nn.sigmoid(gin[0] + gst[0, at, :])
        update = jax.nn.sigmoid(gin[1] + gst[1, at, :])
        cand = jnp.tanh(gin[2] + reset * gst[2, at, :])
        old = mem[at, pl.ds(pl.multiple_of(m * share, share), share)].astype(F32)
        upd = (1.0 - update) * cand + update * old
        out = jnp.where(cnt[at, :][:, 0:1] > 0.0, upd, old).astype(BF)
        newm[at, :] = out
        new_ref[at, :] = out

    aggregate(0)
    tables()
    ld_win.wait()
    for r in range(1, chunks):
        aggregate(r)
        gates(r - 1)
    gates(chunks - 1)

    def state_copy(d, s):
        return pltpu.make_async_remote_copy(
            src_ref=st_send.at[pl.ds(pl.multiple_of(d * scap, scap), scap), :],
            dst_ref=st_recv.at[pl.ds(pl.multiple_of(s * scap, scap), scap), :],
            send_sem=ss_sem.at[d], recv_sem=sr_sem.at[s],
            device_id=(d, m), device_id_type=MESH,
        )

    st_send[...] = dot(smat[...], newm[...]).astype(BF)

    def send_state(k, c):
        state_copy((me + k) % n, me).start()
        return c

    lax.fori_loop(1, n, send_state, 0)
    mine = pl.ds(pl.multiple_of(me * scap, scap), scap)
    st_recv[mine, :] = st_send[mine, :]
    ld_ws.wait()
    selfp[...] = dot(dot(qmat[...], newm[...]).astype(BF), ws[...])
    ld_wn.wait()

    def recv_state(k, c):
        s = (me - k + n) % n
        state_copy(s, s).wait_recv()
        return c

    lax.fori_loop(1, n, recv_state, 0)

    def rs_copy(j, to):
        return pltpu.make_async_remote_copy(
            src_ref=rs_send.at[j], dst_ref=rs_recv.at[j],
            send_sem=rs_ssem.at[j], recv_sem=rs_rsem.at[j],
            device_id=(me, to), device_id_type=MESH,
        )

    def embed(b0, b1):
        ats = [pl.ds(pl.multiple_of(b * qblock, qblock), qblock) for b in (b0, b1)]
        tally = jnp.concatenate([cmat[at, :] for at in ats], axis=0)
        mean = (dot(tally, st_recv[...]) / float(neigh_ref.shape[0])).astype(BF)
        out = dot(mean, wn[...])
        return out[:qblock] + selfp[ats[0], :], out[qblock:] + selfp[ats[1], :]

    to_core = [rs_copy(0, core), rs_copy(1, core)]
    to_cross = rs_copy(2, cross)
    part0, part1 = embed(far, core)
    rs_send[0] = part0.astype(BF)
    to_core[0].start()
    rs_send[1] = part1.astype(BF)
    to_core[1].start()
    part0, part1 = embed(cross, m)
    to_core[0].wait_recv()
    rs_send[2] = (part0 + rs_recv[0].astype(F32)).astype(BF)
    to_cross.start()
    to_core[1].wait_recv()
    part1 = part1 + rs_recv[1].astype(F32) + b_emb_ref[...]
    to_cross.wait_recv()
    emb_ref[...] = jnp.maximum(part1 + rs_recv[2].astype(F32), 0.0).astype(BF)

    def drain(s, c):
        relay(m, s, cross, xs_sem, xr_sem).wait_send()
        relay(m, s, core, c1s_sem, c1r_sem).wait_send()
        relay(cross, s, core, c2s_sem, c2r_sem).wait_send()
        return c

    lax.fori_loop(0, n, drain, 0)

    def drain_peers(k, c):
        d = (me + k) % n
        for cp in dispatch_copies(d, me):
            cp.wait_send()
        state_copy(d, me).wait_send()
        return c

    lax.fori_loop(1, n, drain_peers, 0)
    for cp in stage1 + stage2 + stage3 + to_core + [to_cross]:
        cp.wait_send()


def hand_over(new_in, emb_in, new_out, emb_out, sem):
    copies = [
        pltpu.make_async_copy(new_in, new_out, sem.at[0]),
        pltpu.make_async_copy(emb_in, emb_out, sem.at[1]),
    ]
    for c in copies:
        c.start()
    for c in copies:
        c.wait()


def per_device(
    event_feats, event_owner, event_slot, memory, w_msg_event, w_msg_state, b_msg, w_msg_out,
    b_out, w_input, w_hidden, b_input, b_hidden, state_slots, neighbours, query_slots,
    w_neigh, w_self, b_embed,
):
    n = lax.axis_size("nodes")
    shares = lax.axis_size("mp")
    assert shares == 4
    events, feat = event_feats.shape
    nodes, width = memory.shape
    cap = 2 * events // n
    share = width // shares
    hid = w_msg_event.shape[1]
    half = width // 2
    scap = state_slots.shape[1]
    queries = query_slots.shape[0]
    qblock = queries // shares
    fcols = feat // shares
    vm = pl.BlockSpec(memory_space=pltpu.VMEM)
    hbm = pl.BlockSpec(memory_space=pl.ANY)
    V = pltpu.VMEM
    dma = lambda k: pltpu.SemaphoreType.DMA((k,))
    scratch = [
        V((1, events), jnp.int32), V((1, events), jnp.int32), V((1, hid), F32),
        V((1, width), F32), V(b_input.shape, F32), V(b_hidden.shape, F32),
        V(state_slots.shape, jnp.int32), V(neighbours.shape[::-1], jnp.int32),
        V((1, queries), jnp.int32), V((1, width), F32),
        V((events, fcols), BF), V(memory.shape, BF), V(w_msg_event.shape, BF),
        V(w_msg_state.shape, BF), V(w_msg_out.shape, BF), V(w_input.shape, BF),
        V(w_hidden.shape, BF), V(w_neigh.shape, BF), V(w_self.shape, BF),
        V((1, events), F32), V((events, LANES), BF), V((n, cap, fcols), BF),
        V((n, 1, cap), F32), V((4, n, cap, fcols), BF), V((n, 1, cap), F32),
        V((nodes, hid), BF), V((3, nodes, share), F32),
        V((nodes, hid), F32), V((nodes, LANES), F32),
        V((nodes, half), BF), V((nodes, half), BF), V((nodes, half), F32),
        V((nodes, half), BF), V((nodes, half), BF), V((nodes, half), BF), V((nodes, half), BF),
        V((n * scap, nodes), BF), V((queries, n * scap), BF), V((queries, nodes), BF),
        V((nodes, share), BF), V((n * scap, share), BF), V((n * scap, share), BF),
        V((queries, width), F32), V((3, qblock, width), BF), V((3, qblock, width), BF),
        dma(19), dma(n), dma(n), dma(n), dma(n), dma(n), dma(n),
        dma(n), dma(n), dma(n), dma(n), dma(3 * AR_CHUNKS), dma(3 * AR_CHUNKS), dma(n), dma(n), dma(3), dma(3),
    ]
    results = pl.pallas_call(
        functools.partial(kernel, n),
        out_shape=(
            jax.ShapeDtypeStruct((nodes, share), BF),
            jax.ShapeDtypeStruct((qblock, width), BF),
        ),
        in_specs=[hbm] * 19,
        out_specs=(vm, vm),
        scratch_shapes=scratch,
        compiler_params=pltpu.CompilerParams(
            collective_id=0, has_side_effects=True, vmem_limit_bytes=VMEM_BYTES
        ),
        cost_estimate=pl.CostEstimate(flops=8_000_000_000, bytes_accessed=9_000_000, transcendentals=0),
    )(
        event_owner.reshape(1, events), event_slot.reshape(1, events), b_msg.reshape(1, -1),
        b_out.reshape(1, -1), b_input, b_hidden, state_slots, neighbours.T,
        query_slots.reshape(1, -1), b_embed.reshape(1, -1),
        event_feats, memory, w_msg_event, w_msg_state, w_msg_out, w_input, w_hidden,
        w_neigh, w_self,
    )
    return pl.pallas_call(
        hand_over,
        out_shape=[jax.ShapeDtypeStruct(r.shape, r.dtype) for r in results],
        in_specs=[hbm, hbm],
        out_specs=[hbm, hbm],
        scratch_shapes=[dma(2)],
        compiler_params=pltpu.CompilerParams(vmem_limit_bytes=VMEM_BYTES),
    )(*results)


def solution(mesh):
    in_specs = (
        P("nodes", None),
        P("nodes", None),
        P("nodes"),
        P("nodes", None),
        P(None, "mp"),
        P(None, "mp"),
        P("mp"),
        P("mp", None),
        P(),
        P(None, None, "mp"),
        P(None, None, "mp"),
        P(None, "mp"),
        P(None, "mp"),
        P("nodes", None),
        P("nodes", None),
        P("nodes"),
        P("mp", None),
        P("mp", None),
        P(),
    )
    out_specs = (P("nodes", "mp"), P(("nodes", "mp"), None))
    return jax.shard_map(
        per_device, mesh=mesh, in_specs=in_specs, out_specs=out_specs, check_vma=False
    )
```

```python
import functools

import jax
import jax.numpy as jnp
from jax import lax
from jax.experimental import pallas as pl
from jax.experimental.pallas import tpu as pltpu
from jax.sharding import PartitionSpec as P

BF = jnp.bfloat16
F32 = jnp.float32
MESH = pl.DeviceIdType.MESH
LANES = 128
AR_CHUNKS = 4
VMEM_BYTES = 60 * 1024 * 1024


def iota(shape, dim):
    return lax.broadcasted_iota(jnp.int32, shape, dim)


def fiota(shape, dim):
    return iota(shape, dim).astype(F32)


def ones_where(cond):
    return jnp.where(cond, 1.0, 0.0)


def to_col(row):
    size = row.shape[1]
    eye = iota((size, size), 0) == iota((size, size), 1)
    return jnp.sum(jnp.where(eye, row, 0.0), axis=1, keepdims=True)


def to_row(col):
    size = col.shape[0]
    eye = iota((size, size), 0) == iota((size, size), 1)
    return jnp.sum(jnp.where(eye, col, 0.0), axis=0, keepdims=True)


def dot(a, b):
    return jnp.dot(a, b, preferred_element_type=F32)


def kernel(
    n,
    owner_hbm, slot_hbm, b_msg_hbm, b_out_hbm, b_in_hbm, b_hid_hbm,
    sslots_hbm, neigh_hbm, query_hbm, b_emb_hbm,
    feats_hbm, mem_hbm, wev_hbm, wst_hbm, wout_hbm, win_hbm, whid_hbm, wn_hbm, ws_hbm,
    new_ref, emb_ref,
    owner_ref, slot_ref, b_msg_ref, b_out_ref, b_in_ref, b_hid_ref,
    sslots_ref, neigh_ref, query_ref, b_emb_ref,
    feats, mem, wev, wst, wout, win, whid, wn, ws,
    target, send_buf, ids_send, arr, ids, gst,
    acc, cnt, ar_s1, ar_r1, p_own, ar_s2, ar_r2, agg_own, agg_oth,
    smat, cmat, qmat, newm, st_send, st_recv, selfp, rs_send, rs_recv,
    load_sem, ds_sem, dr_sem, is_sem, ir_sem, xs_sem, xr_sem,
    c1s_sem, c1r_sem, c2s_sem, c2r_sem, ar_ssem, ar_rsem, ss_sem, sr_sem, rs_ssem, rs_rsem,
):
    me = lax.axis_index("nodes")
    m = lax.axis_index("mp")
    core = m + 1 - 2 * (m % 2)
    cross = (m + 2) % 4
    far = (core + 2) % 4
    events = owner_hbm.shape[1]
    cap = ids.shape[2]
    sc = cap // 4
    nodes = mem.shape[0]
    width = mem.shape[1]
    share = width // 4
    half = width // 2
    scap = sslots_ref.shape[1]
    qblock = emb_ref.shape[0]
    feat = feats.shape[1]

    loads = []

    def load(src, dst):
        c = pltpu.make_async_copy(src, dst, load_sem.at[len(loads)])
        c.start()
        loads.append(c)
        return c

    ld_owner = load(owner_hbm, owner_ref)
    ld_slot = load(slot_hbm, slot_ref)
    ld_feats = load(feats_hbm, feats)

    barrier = pltpu.get_barrier_semaphore()

    def greet(k, c):
        pl.semaphore_signal(barrier, inc=1, device_id=((me + k) % n, m), device_id_type=MESH)
        return c

    lax.fori_loop(1, n, greet, 0)
    pl.semaphore_signal(barrier, inc=1, device_id=(me, core), device_id_type=MESH)
    pl.semaphore_signal(barrier, inc=1, device_id=(me, cross), device_id_type=MESH)

    ld_owner.wait()
    ld_slot.wait()
    ld_mem = load(mem_hbm, mem)
    ld_wst = load(wst_hbm, wst)
    ld_b_msg = load(b_msg_hbm, b_msg_ref)
    ld_wev = load(wev_hbm, wev.at[0:feat, :])
    ld_wout = load(wout_hbm, wout)
    ld_whid = load(whid_hbm, whid)
    ld_win = load(win_hbm, win)
    ld_small = [
        load(b_hid_hbm, b_hid_ref), load(sslots_hbm, sslots_ref), load(neigh_hbm, neigh_ref),
        load(query_hbm, query_ref), load(b_out_hbm, b_out_ref), load(b_in_hbm, b_in_ref),
        load(b_emb_hbm, b_emb_ref),
    ]
    ld_ws = load(ws_hbm, ws)
    ld_wn = load(wn_hbm, wn)
    rows = max(n, 16)
    oi = iota((rows, LANES), 0)
    tri = ones_where(iota((LANES, LANES), 0) < iota((LANES, LANES), 1)).astype(BF)
    running = jnp.zeros((rows, 1), F32)
    for j in range(events // LANES):
        at = slice(j * LANES, (j + 1) * LANES)
        ow = owner_ref[:, at]
        match = ones_where(ow == oi)
        before = dot(match.astype(BF), tri) + running
        place = jnp.sum(match * before, axis=0, keepdims=True)
        target[:, at] = ow.astype(F32) * float(cap) + place
        running = running + jnp.sum(match, axis=1, keepdims=True)

    pl.semaphore_wait(barrier, n + 1)
    ld_feats.wait()

    def event_copy(d, s):
        return pltpu.make_async_remote_copy(
            src_ref=send_buf.at[d], dst_ref=arr.at[m, s],
            send_sem=ds_sem.at[d], recv_sem=dr_sem.at[s],
            device_id=(d, m), device_id_type=MESH,
        )

    def id_copy(d, s):
        return pltpu.make_async_remote_copy(
            src_ref=ids_send.at[d], dst_ref=ids.at[s],
            send_sem=is_sem.at[d], recv_sem=ir_sem.at[s],
            device_id=(d, m), device_id_type=MESH,
        )

    def relay(src_col, s, to, ssem, rsem):
        return pltpu.make_async_remote_copy(
            src_ref=arr.at[src_col, s], dst_ref=arr.at[src_col, s],
            send_sem=ssem.at[s], recv_sem=rsem.at[s],
            device_id=(me, to), device_id_type=MESH,
        )

    mid = n // 2
    here, place_in = me // mid, me % mid
    there = (here + 1) % 2

    def source(u):
        far_side = u // mid
        return ((here + far_side) % 2) * mid + (place_in - u % mid + mid) % mid

    def build(half_at):
        count = mid * sc
        i = iota((count, 1), 0)
        wanted = (half_at * mid + i // sc) * cap + m * sc + i % sc
        pick = ones_where(target[...] == wanted.astype(F32)).astype(BF)
        built = dot(pick, feats[...]).reshape(mid, sc, feat)
        send_buf[pl.ds(half_at * mid, mid)] = built.astype(BF)

    def build_ids():
        groups = cap // 16
        goal = target[...]
        high = jnp.floor(goal * (1.0 / 16.0))
        low = goal - 16.0 * high
        slot = slot_ref[...].astype(F32) + 1.0
        left = jnp.where(high == fiota((n * groups, events), 0), slot, 0.0).astype(BF)
        right = ones_where(low == fiota((16, events), 0)).astype(BF)
        digits = lax.dot_general(
            left, right, (((1,), (1,)), ((), ())), preferred_element_type=F32
        ).astype(BF)
        lane = iota((16, cap), 1)
        spread = dot(digits, ones_where(lane % 16 == iota((16, cap), 0)).astype(BF))
        wide = (n * groups, cap)
        keep = jnp.where(iota(wide, 1) // 16 == iota(wide, 0) % groups, spread, 0.0).astype(BF)
        tall = (rows, n * groups)
        table = dot(ones_where(iota(tall, 1) // groups == iota(tall, 0)).astype(BF), keep)
        for d in range(n):
            ids_send[d] = table[d:d + 1, :]

    def pass_on(u):
        s = source(u)
        relay(m, s, cross, xs_sem, xr_sem).start()
        relay(m, s, core, c1s_sem, c1r_sem).start()

    def arrive(u):
        s = source(u)
        event_copy(s, s).wait_recv()
        id_copy(s, s).wait_recv()
        pass_on(u)

    def forward(u):
        s = source(u)
        relay(cross, s, cross, xs_sem, xr_sem).wait_recv()
        relay(cross, s, core, c2s_sem, c2r_sem).start()

    def whole(block):
        return block if sc % 16 == 0 else block.astype(F32)

    def absorb(*turns):
        xs, ohs, ohts = [], [], []
        for u in turns:
            s = source(u)
            relay(core, s, core, c1s_sem, c1r_sem).wait_recv()
            relay(far, s, core, c2s_sem, c2r_sem).wait_recv()
            xs += [whole(arr[j, s]) for j in range(4)]
            row = ids[s]
            ohs.append(ones_where(to_col(row) == fiota((cap, nodes), 1) + 1.0).astype(BF))
            oht = ones_where(row == fiota((nodes, cap), 0) + 1.0)
            for lo in range(0, cap, LANES):
                wide = min(cap, LANES)
                cnt[:, 0:wide] += oht[:, lo:lo + wide]
            ohts.append(oht.astype(BF))
        x = jnp.concatenate([jnp.concatenate(xs, axis=0).astype(BF), jnp.concatenate(ohs, axis=0)], axis=1)
        hidden = jnp.maximum(dot(x, wev[...]), 0.0).astype(BF)
        if cap % LANES == 0:
            acc[...] += dot(jnp.concatenate(ohts, axis=1), hidden)
        else:
            for k, oht in enumerate(ohts):
                acc[...] += dot(oht, hidden[k * cap:(k + 1) * cap])

    build(there)

    def start_there(j, c):
        event_copy(there * mid + (place_in + j) % mid, me).start()
        return c

    lax.fori_loop(0, mid, start_there, 0)
    build(here)
    arr[m, me] = send_buf[me]
    pass_on(0)

    def start_here(j, c):
        event_copy(here * mid + (place_in + j) % mid, me).start()
        return c

    lax.fori_loop(1, mid, start_here, 0)
    build_ids()

    def start_ids(k, c):
        id_copy((me + k) % n, me).start()
        return c

    lax.fori_loop(1, n, start_ids, 0)
    ids[me] = ids_send[me]

    acc[...] = jnp.zeros_like(acc)
    cnt[...] = jnp.zeros_like(cnt)
    ld_mem.wait()
    ld_wst.wait()
    ld_b_msg.wait()
    wev[pl.ds(feat, nodes), :] = (dot(mem[...], wst[...]) + b_msg_ref[...]).astype(BF)
    ld_wev.wait()

    def each(body):
        def run(u, c):
            body(u)
            return c

        return run

    lax.fori_loop(1, mid, each(arrive), 0)

    def early(p):
        forward(2 * p)
        forward(2 * p + 1)
        absorb(2 * p, 2 * p + 1)
        arrive(mid + p)

    def late(u):
        forward(u - 1)
        absorb(u - 1)
        arrive(u)

    lax.fori_loop(0, mid // 2, each(early), 0)
    first = mid + mid // 2
    lax.fori_loop(mid, first - 1, each(forward), 0)
    lax.fori_loop(mid, first - 1, each(absorb), 0)
    lax.fori_loop(first, n, each(late), 0)
    forward(n - 1)
    absorb(n - 1)

    ld_wout.wait()
    chunks = AR_CHUNKS
    crows = nodes // chunks
    my_half = pl.ds(pl.multiple_of((m % 2) * half, half), half)
    its_half = pl.ds(pl.multiple_of((core % 2) * half, half), half)

    def ar_copy(stage, r, src, dst, to):
        at = pl.ds(r * crows, crows)
        return pltpu.make_async_remote_copy(
            src_ref=src.at[at, :], dst_ref=dst.at[at, :],
            send_sem=ar_ssem.at[stage * chunks + r], recv_sem=ar_rsem.at[stage * chunks + r],
            device_id=(me, to), device_id_type=MESH,
        )

    def sum_out(r, cols):
        at = pl.ds(r * crows, crows)
        return dot(acc[at, :].astype(BF), wout[:, cols])

    stage1 = [ar_copy(0, r, ar_s1, ar_r1, core) for r in range(chunks)]
    stage2 = [ar_copy(1, r, ar_s2, ar_r2, cross) for r in range(chunks)]
    stage3 = [ar_copy(2, r, agg_own, agg_oth, core) for r in range(chunks)]
    for r in range(chunks):
        at = pl.ds(r * crows, crows)
        ar_s1[at, :] = sum_out(r, its_half).astype(BF)
        stage1[r].start()
    for r in range(chunks):
        at = pl.ds(r * crows, crows)
        own = sum_out(r, my_half)
        stage1[r].wait_recv()
        own = own + ar_r1[at, :].astype(F32)
        p_own[at, :] = own
        ar_s2[at, :] = own.astype(BF)
        stage2[r].start()

    ld_whid.wait()
    for ld in ld_small:
        ld.wait()
    for g in range(3):
        gst[g] = dot(mem[...], whid[g]) + b_hid_ref[g:g + 1, :]
    cnt[...] = jnp.broadcast_to(jnp.sum(cnt[...], axis=1, keepdims=True), cnt.shape)

    def tables():
        place = iota((cmat.shape[1], cmat.shape[0]), 0)
        total = jnp.zeros((cmat.shape[1], cmat.shape[0]), F32)
        for k in range(neigh_ref.shape[0]):
            total = total + ones_where(neigh_ref[k:k + 1, :] == place)
        cmat[...] = total.T.astype(BF)
        qcol = to_col(query_ref[...].astype(F32))
        qmat[...] = ones_where(qcol == fiota(qmat.shape, 1)).astype(BF)

        def fill(d, c):
            col = to_col(sslots_ref[pl.ds(d, 1), :].astype(F32))
            smat[pl.ds(pl.multiple_of(d * scap, scap), scap), :] = ones_where(
                col == fiota((scap, nodes), 1)
            ).astype(BF)
            return c

        lax.fori_loop(0, n, fill, 0)

    def aggregate(r):
        at = pl.ds(r * crows, crows)
        stage2[r].wait_recv()
        total = p_own[at, :] + ar_r2[at, :].astype(F32)
        agg = total / jnp.maximum(cnt[at, :][:, 0:1], 1.0) + b_out_ref[:, my_half]
        agg_own[at, :] = agg.astype(BF)
        stage3[r].start()

    def gates(r):
        at = pl.ds(r * crows, crows)
        mine = [dot(agg_own[at, :], win[g, my_half, :]) for g in range(3)]
        stage3[r].wait_recv()
        gin = [
            mine[g] + dot(agg_oth[at, :], win[g, its_half, :]) + b_in_ref[g:g + 1, :]
            for g in range(3)
        ]
        reset = jax.nn.sigmoid(gin[0] + gst[0, at, :])
        update = jax.nn.sigmoid(gin[1] + gst[1, at, :])
        cand = jnp.tanh(gin[2] + reset * gst[2, at, :])
        old = mem[at, pl.ds(pl.multiple_of(m * share, share), share)].astype(F32)
        upd = (1.0 - update) * cand + update * old
        out = jnp.where(cnt[at, :][:, 0:1] > 0.0, upd, old).astype(BF)
        newm[at, :] = out
        new_ref[at, :] = out

    aggregate(0)
    tables()
    ld_win.wait()
    for r in range(1, chunks):
        aggregate(r)
        gates(r - 1)
    gates(chunks - 1)

    def state_copy(d, s):
        return pltpu.make_async_remote_copy(
            src_ref=st_send.at[pl.ds(pl.multiple_of(d * scap, scap), scap), :],
            dst_ref=st_recv.at[pl.ds(pl.multiple_of(s * scap, scap), scap), :],
            send_sem=ss_sem.at[d], recv_sem=sr_sem.at[s],
            device_id=(d, m), device_id_type=MESH,
        )

    st_send[...] = dot(smat[...], newm[...]).astype(BF)

    def send_state(k, c):
        state_copy((me + k) % n, me).start()
        return c

    lax.fori_loop(1, n, send_state, 0)
    mine = pl.ds(pl.multiple_of(me * scap, scap), scap)
    st_recv[mine, :] = st_send[mine, :]
    ld_ws.wait()
    selfp[...] = dot(dot(qmat[...], newm[...]).astype(BF), ws[...])
    ld_wn.wait()

    def recv_state(k, c):
        s = (me - k + n) % n
        state_copy(s, s).wait_recv()
        return c

    lax.fori_loop(1, n, recv_state, 0)

    def rs_copy(j, to):
        return pltpu.make_async_remote_copy(
            src_ref=rs_send.at[j], dst_ref=rs_recv.at[j],
            send_sem=rs_ssem.at[j], recv_sem=rs_rsem.at[j],
            device_id=(me, to), device_id_type=MESH,
        )

    def embed(b0, b1):
        ats = [pl.ds(pl.multiple_of(b * qblock, qblock), qblock) for b in (b0, b1)]
        tally = jnp.concatenate([cmat[at, :] for at in ats], axis=0)
        mean = (dot(tally, st_recv[...]) / float(neigh_ref.shape[0])).astype(BF)
        out = dot(mean, wn[...])
        return out[:qblock] + selfp[ats[0], :], out[qblock:] + selfp[ats[1], :]

    to_core = [rs_copy(0, core), rs_copy(1, core)]
    to_cross = rs_copy(2, cross)
    part0, part1 = embed(far, core)
    rs_send[0] = part0.astype(BF)
    to_core[0].start()
    rs_send[1] = part1.astype(BF)
    to_core[1].start()
    part0, part1 = embed(cross, m)
    to_core[0].wait_recv()
    rs_send[2] = (part0 + rs_recv[0].astype(F32)).astype(BF)
    to_cross.start()
    to_core[1].wait_recv()
    part1 = part1 + rs_recv[1].astype(F32) + b_emb_ref[...]
    to_cross.wait_recv()
    emb_ref[...] = jnp.maximum(part1 + rs_recv[2].astype(F32), 0.0).astype(BF)

    def drain(s, c):
        relay(m, s, cross, xs_sem, xr_sem).wait_send()
        relay(m, s, core, c1s_sem, c1r_sem).wait_send()
        relay(cross, s, core, c2s_sem, c2r_sem).wait_send()
        return c

    lax.fori_loop(0, n, drain, 0)

    def drain_peers(k, c):
        d = (me + k) % n
        event_copy(d, me).wait_send()
        id_copy(d, me).wait_send()
        state_copy(d, me).wait_send()
        return c

    lax.fori_loop(1, n, drain_peers, 0)
    for cp in stage1 + stage2 + stage3 + to_core + [to_cross]:
        cp.wait_send()


def per_device(
    event_feats, event_owner, event_slot, memory, w_msg_event, w_msg_state, b_msg, w_msg_out,
    b_out, w_input, w_hidden, b_input, b_hidden, state_slots, neighbours, query_slots,
    w_neigh, w_self, b_embed,
):
    n = lax.axis_size("nodes")
    shares = lax.axis_size("mp")
    assert shares == 4
    events, feat = event_feats.shape
    nodes, width = memory.shape
    cap = 2 * events // n
    share = width // shares
    hid = w_msg_event.shape[1]
    half = width // 2
    scap = state_slots.shape[1]
    queries = query_slots.shape[0]
    qblock = queries // shares
    vm = pl.BlockSpec(memory_space=pltpu.VMEM)
    hbm = pl.BlockSpec(memory_space=pl.ANY)
    V = pltpu.VMEM
    dma = lambda k: pltpu.SemaphoreType.DMA((k,))
    scratch = [
        V((1, events), jnp.int32), V((1, events), jnp.int32), V((1, hid), F32),
        V((1, width), F32), V(b_input.shape, F32), V(b_hidden.shape, F32),
        V(state_slots.shape, jnp.int32), V(neighbours.shape[::-1], jnp.int32),
        V((1, queries), jnp.int32), V((1, width), F32),
        V((events, feat), BF), V(memory.shape, BF), V((feat + nodes, hid), BF),
        V(w_msg_state.shape, BF), V(w_msg_out.shape, BF), V(w_input.shape, BF),
        V(w_hidden.shape, BF), V(w_neigh.shape, BF), V(w_self.shape, BF),
        V((1, events), F32), V((n, cap // 4, feat), BF),
        V((n, 1, cap), F32), V((4, n, cap // 4, feat), BF), V((n, 1, cap), F32),
        V((3, nodes, share), F32),
        V((nodes, hid), F32), V((nodes, LANES), F32),
        V((nodes, half), BF), V((nodes, half), BF), V((nodes, half), F32),
        V((nodes, half), BF), V((nodes, half), BF), V((nodes, half), BF), V((nodes, half), BF),
        V((n * scap, nodes), BF), V((queries, n * scap), BF), V((queries, nodes), BF),
        V((nodes, share), BF), V((n * scap, share), BF), V((n * scap, share), BF),
        V((queries, width), F32), V((3, qblock, width), BF), V((3, qblock, width), BF),
        dma(19), dma(n), dma(n), dma(n), dma(n), dma(n), dma(n),
        dma(n), dma(n), dma(n), dma(n), dma(3 * AR_CHUNKS), dma(3 * AR_CHUNKS), dma(n), dma(n), dma(3), dma(3),
    ]
    return pl.pallas_call(
        functools.partial(kernel, n),
        out_shape=(
            jax.ShapeDtypeStruct((nodes, share), BF),
            jax.ShapeDtypeStruct((qblock, width), BF),
        ),
        in_specs=[hbm] * 19,
        out_specs=(vm, vm),
        scratch_shapes=scratch,
        compiler_params=pltpu.CompilerParams(
            collective_id=0, has_side_effects=True, vmem_limit_bytes=VMEM_BYTES
        ),
        cost_estimate=pl.CostEstimate(flops=8_000_000_000, bytes_accessed=9_000_000, transcendentals=0),
    )(
        event_owner.reshape(1, events), event_slot.reshape(1, events), b_msg.reshape(1, -1),
        b_out.reshape(1, -1), b_input, b_hidden, state_slots, neighbours.T,
        query_slots.reshape(1, -1), b_embed.reshape(1, -1),
        event_feats, memory, w_msg_event, w_msg_state, w_msg_out, w_input, w_hidden,
        w_neigh, w_self,
    )

def solution(mesh):
    in_specs = (
        P("nodes", None),
        P("nodes", None),
        P("nodes"),
        P("nodes", None),
        P(None, "mp"),
        P(None, "mp"),
        P("mp"),
        P("mp", None),
        P(),
        P(None, None, "mp"),
        P(None, None, "mp"),
        P(None, "mp"),
        P(None, "mp"),
        P("nodes", None),
        P("nodes", None),
        P("nodes"),
        P("mp", None),
        P("mp", None),
        P(),
    )
    out_specs = (P("nodes", "mp"), P(("nodes", "mp"), None))
    return jax.shard_map(
        per_device, mesh=mesh, in_specs=in_specs, out_specs=out_specs, check_vma=False
    )
```

```python
import functools

import jax
import jax.numpy as jnp
from jax import lax
from jax.experimental import pallas as pl
from jax.experimental.pallas import tpu as pltpu
from jax.sharding import PartitionSpec as P

BF = jnp.bfloat16
F32 = jnp.float32
MESH = pl.DeviceIdType.MESH
LANES = 128
AR_CHUNKS = 4
VMEM_BYTES = 60 * 1024 * 1024


def iota(shape, dim):
    return lax.broadcasted_iota(jnp.int32, shape, dim)


def fiota(shape, dim):
    return iota(shape, dim).astype(F32)


def ones_where(cond):
    return jnp.where(cond, 1.0, 0.0)


def to_col(row):
    size = row.shape[1]
    eye = iota((size, size), 0) == iota((size, size), 1)
    return jnp.sum(jnp.where(eye, row, 0.0), axis=1, keepdims=True)


def to_row(col):
    size = col.shape[0]
    eye = iota((size, size), 0) == iota((size, size), 1)
    return jnp.sum(jnp.where(eye, col, 0.0), axis=0, keepdims=True)


def dot(a, b):
    return jnp.dot(a, b, preferred_element_type=F32)


def kernel(
    n,
    owner_hbm, slot_hbm, b_msg_hbm, b_out_hbm, b_in_hbm, b_hid_hbm,
    sslots_hbm, neigh_hbm, query_hbm, b_emb_hbm,
    feats_hbm, mem_hbm, wev_hbm, wst_hbm, wout_hbm, win_hbm, whid_hbm, wn_hbm, ws_hbm,
    new_ref, emb_ref,
    owner_ref, slot_ref, b_msg_ref, b_out_ref, b_in_ref, b_hid_ref,
    sslots_ref, neigh_ref, query_ref, b_emb_ref,
    feats, mem, wev, wst, wout, win, whid, wn, ws,
    target, slotcol, send_buf, ids_send, arr, ids, proj_ref, gst,
    acc, cnt, ar_s1, ar_r1, p_own, ar_s2, ar_r2, agg_own, agg_oth,
    smat, cmat, qmat, newm, st_send, st_recv, selfp, rs_send, rs_recv,
    load_sem, ds_sem, dr_sem, is_sem, ir_sem, xs_sem, xr_sem,
    c1s_sem, c1r_sem, c2s_sem, c2r_sem, ar_ssem, ar_rsem, ss_sem, sr_sem, rs_ssem, rs_rsem,
):
    me = lax.axis_index("nodes")
    m = lax.axis_index("mp")
    core = m + 1 - 2 * (m % 2)
    cross = (m + 2) % 4
    far = (core + 2) % 4
    events = owner_hbm.shape[1]
    cap = send_buf.shape[1]
    nodes = mem.shape[0]
    width = mem.shape[1]
    share = width // 4
    half = width // 2
    scap = sslots_ref.shape[1]
    qblock = emb_ref.shape[0]
    fcols = feats.shape[1]

    loads = []

    def load(src, dst):
        c = pltpu.make_async_copy(src, dst, load_sem.at[len(loads)])
        c.start()
        loads.append(c)
        return c

    ld_owner = load(owner_hbm, owner_ref)
    ld_slot = load(slot_hbm, slot_ref)
    ld_feats = load(feats_hbm.at[:, pl.ds(pl.multiple_of(m * fcols, fcols), fcols)], feats)

    barrier = pltpu.get_barrier_semaphore()

    def greet(k, c):
        pl.semaphore_signal(barrier, inc=1, device_id=((me + k) % n, m), device_id_type=MESH)
        return c

    lax.fori_loop(1, n, greet, 0)
    pl.semaphore_signal(barrier, inc=1, device_id=(me, core), device_id_type=MESH)
    pl.semaphore_signal(barrier, inc=1, device_id=(me, cross), device_id_type=MESH)

    ld_owner.wait()
    ld_slot.wait()
    ld_mem = load(mem_hbm, mem)
    ld_wst = load(wst_hbm, wst)
    ld_b_msg = load(b_msg_hbm, b_msg_ref)
    ld_wev = load(wev_hbm, wev)
    ld_wout = load(wout_hbm, wout)
    ld_whid = load(whid_hbm, whid)
    ld_win = load(win_hbm, win)
    ld_small = [
        load(b_hid_hbm, b_hid_ref), load(sslots_hbm, sslots_ref), load(neigh_hbm, neigh_ref),
        load(query_hbm, query_ref), load(b_out_hbm, b_out_ref), load(b_in_hbm, b_in_ref),
        load(b_emb_hbm, b_emb_ref),
    ]
    ld_ws = load(ws_hbm, ws)
    ld_wn = load(wn_hbm, wn)
    rows = max(n, 16)
    oi = iota((rows, LANES), 0)
    tri = ones_where(iota((LANES, LANES), 0) < iota((LANES, LANES), 1)).astype(BF)
    running = jnp.zeros((rows, 1), F32)
    for j in range(events // LANES):
        at = slice(j * LANES, (j + 1) * LANES)
        ow = owner_ref[:, at]
        match = ones_where(ow == oi)
        before = dot(match.astype(BF), tri) + running
        place = jnp.sum(match * before, axis=0, keepdims=True)
        target[:, at] = ow.astype(F32) * float(cap) + place
        running = running + jnp.sum(match, axis=1, keepdims=True)
        col = to_col(slot_ref[:, at].astype(F32) + 1.0)
        slotcol[at, :] = jnp.broadcast_to(col, (LANES, LANES)).astype(BF)

    pl.semaphore_wait(barrier, n + 1)
    ld_feats.wait()

    def dispatch_copies(d, s):
        return (
            pltpu.make_async_remote_copy(
                src_ref=send_buf.at[d], dst_ref=arr.at[m, s],
                send_sem=ds_sem.at[d], recv_sem=dr_sem.at[s],
                device_id=(d, m), device_id_type=MESH,
            ),
            pltpu.make_async_remote_copy(
                src_ref=ids_send.at[d], dst_ref=ids.at[s],
                send_sem=is_sem.at[d], recv_sem=ir_sem.at[s],
                device_id=(d, m), device_id_type=MESH,
            ),
        )

    def relay(src_col, s, to, ssem, rsem):
        return pltpu.make_async_remote_copy(
            src_ref=arr.at[src_col, s], dst_ref=arr.at[src_col, s],
            send_sem=ssem.at[s], recv_sem=rsem.at[s],
            device_id=(me, to), device_id_type=MESH,
        )

    mid = n // 2
    here, place_in = me // mid, me % mid
    there = (here + 1) % 2

    def source(u):
        far_side = u // mid
        return ((here + far_side) % 2) * mid + (place_in - u % mid + mid) % mid

    def block_for(d):
        pick = ones_where(
            target[...] == fiota((cap, events), 0) + (d * cap).astype(F32)
        ).astype(BF)
        out = dot(pick, jnp.concatenate([feats[...], slotcol[...]], axis=1))
        return out[:, :fcols].astype(BF), to_row(out[:, fcols:fcols + 1])

    def pass_on(u):
        s = source(u)
        relay(m, s, cross, xs_sem, xr_sem).start()
        relay(m, s, core, c1s_sem, c1r_sem).start()

    def arrive(u):
        s = source(u)
        for cp in dispatch_copies(s, s):
            cp.wait_recv()
        pass_on(u)

    def forward(u):
        s = source(u)
        relay(cross, s, cross, xs_sem, xr_sem).wait_recv()
        relay(cross, s, core, c2s_sem, c2r_sem).start()

    def absorb(u):
        s = source(u)
        relay(core, s, core, c1s_sem, c1r_sem).wait_recv()
        relay(far, s, core, c2s_sem, c2r_sem).wait_recv()
        x = jnp.concatenate([arr[j, s] for j in range(4)], axis=1)
        row = ids[s]
        oh = ones_where(to_col(row) == fiota((cap, nodes), 1) + 1.0).astype(BF)
        oht = ones_where(row == fiota((nodes, cap), 0) + 1.0)
        pre = dot(x, wev[...]) + dot(oh, proj_ref[...])
        hidden = jnp.maximum(pre, 0.0).astype(BF)
        acc[...] += dot(oht.astype(BF), hidden)
        for lo in range(0, cap, LANES):
            wide = min(cap, LANES)
            cnt[:, 0:wide] += oht[:, lo:lo + wide]

    def send_block(t):
        d = ((here + t % 2) % 2) * mid + (place_in + t // 2) % mid
        block, idrow = block_for(d)
        send_buf[d] = block
        ids_send[d] = idrow
        for cp in dispatch_copies(d, me):
            cp.start()

    block, idrow = block_for(me)
    arr[m, me] = block
    ids[me] = idrow
    pass_on(0)

    def dispatch(t, c):
        send_block(t)

        @pl.when(jnp.logical_and(t >= 4, t % 2 == 0))
        def _():
            arrive(t // 2 - 1)

        return c

    lax.fori_loop(1, n, dispatch, 0)

    acc[...] = jnp.zeros_like(acc)
    cnt[...] = jnp.zeros_like(cnt)
    ld_mem.wait()
    ld_wst.wait()
    ld_b_msg.wait()
    proj_ref[...] = (dot(mem[...], wst[...]) + b_msg_ref[...]).astype(BF)
    ld_wev.wait()
    def each(body):
        def run(u, c):
            body(u)
            return c

        return run

    lax.fori_loop(0, mid - 3, each(forward), 0)
    lax.fori_loop(0, mid - 4, each(absorb), 0)

    def step(i):
        arrive(i)
        forward(i - 2)
        absorb(i - 3)

    lax.fori_loop(mid - 1, n, each(step), 0)
    forward(n - 2)
    absorb(n - 3)
    forward(n - 1)
    absorb(n - 2)
    absorb(n - 1)

    ld_wout.wait()
    chunks = AR_CHUNKS
    crows = nodes // chunks
    my_half = pl.ds(pl.multiple_of((m % 2) * half, half), half)
    its_half = pl.ds(pl.multiple_of((core % 2) * half, half), half)

    def ar_copy(stage, r, src, dst, to):
        at = pl.ds(r * crows, crows)
        return pltpu.make_async_remote_copy(
            src_ref=src.at[at, :], dst_ref=dst.at[at, :],
            send_sem=ar_ssem.at[stage * chunks + r], recv_sem=ar_rsem.at[stage * chunks + r],
            device_id=(me, to), device_id_type=MESH,
        )

    def sum_out(r, cols):
        at = pl.ds(r * crows, crows)
        return dot(acc[at, :].astype(BF), wout[:, cols])

    stage1 = [ar_copy(0, r, ar_s1, ar_r1, core) for r in range(chunks)]
    stage2 = [ar_copy(1, r, ar_s2, ar_r2, cross) for r in range(chunks)]
    stage3 = [ar_copy(2, r, agg_own, agg_oth, core) for r in range(chunks)]
    for r in range(chunks):
        at = pl.ds(r * crows, crows)
        ar_s1[at, :] = sum_out(r, its_half).astype(BF)
        stage1[r].start()
    for r in range(chunks):
        at = pl.ds(r * crows, crows)
        own = sum_out(r, my_half)
        stage1[r].wait_recv()
        own = own + ar_r1[at, :].astype(F32)
        p_own[at, :] = own
        ar_s2[at, :] = own.astype(BF)
        stage2[r].start()

    ld_whid.wait()
    for ld in ld_small:
        ld.wait()
    for g in range(3):
        gst[g] = dot(mem[...], whid[g]) + b_hid_ref[g:g + 1, :]
    cnt[...] = jnp.broadcast_to(jnp.sum(cnt[...], axis=1, keepdims=True), cnt.shape)

    def tables():
        place = iota((cmat.shape[1], cmat.shape[0]), 0)
        total = jnp.zeros((cmat.shape[1], cmat.shape[0]), F32)
        for k in range(neigh_ref.shape[0]):
            total = total + ones_where(neigh_ref[k:k + 1, :] == place)
        cmat[...] = total.T.astype(BF)
        qcol = to_col(query_ref[...].astype(F32))
        qmat[...] = ones_where(qcol == fiota(qmat.shape, 1)).astype(BF)

        def fill(d, c):
            col = to_col(sslots_ref[pl.ds(d, 1), :].astype(F32))
            smat[pl.ds(pl.multiple_of(d * scap, scap), scap), :] = ones_where(
                col == fiota((scap, nodes), 1)
            ).astype(BF)
            return c

        lax.fori_loop(0, n, fill, 0)

    def aggregate(r):
        at = pl.ds(r * crows, crows)
        stage2[r].wait_recv()
        total = p_own[at, :] + ar_r2[at, :].astype(F32)
        agg = total / jnp.maximum(cnt[at, :][:, 0:1], 1.0) + b_out_ref[:, my_half]
        agg_own[at, :] = agg.astype(BF)
        stage3[r].start()

    def gates(r):
        at = pl.ds(r * crows, crows)
        mine = [dot(agg_own[at, :], win[g, my_half, :]) for g in range(3)]
        stage3[r].wait_recv()
        gin = [
            mine[g] + dot(agg_oth[at, :], win[g, its_half, :]) + b_in_ref[g:g + 1, :]
            for g in range(3)
        ]
        reset = jax.nn.sigmoid(gin[0] + gst[0, at, :])
        update = jax.nn.sigmoid(gin[1] + gst[1, at, :])
        cand = jnp.tanh(gin[2] + reset * gst[2, at, :])
        old = mem[at, pl.ds(pl.multiple_of(m * share, share), share)].astype(F32)
        upd = (1.0 - update) * cand + update * old
        out = jnp.where(cnt[at, :][:, 0:1] > 0.0, upd, old).astype(BF)
        newm[at, :] = out
        new_ref[at, :] = out

    aggregate(0)
    tables()
    ld_win.wait()
    for r in range(1, chunks):
        aggregate(r)
        gates(r - 1)
    gates(chunks - 1)

    def state_copy(d, s):
        return pltpu.make_async_remote_copy(
            src_ref=st_send.at[pl.ds(pl.multiple_of(d * scap, scap), scap), :],
            dst_ref=st_recv.at[pl.ds(pl.multiple_of(s * scap, scap), scap), :],
            send_sem=ss_sem.at[d], recv_sem=sr_sem.at[s],
            device_id=(d, m), device_id_type=MESH,
        )

    st_send[...] = dot(smat[...], newm[...]).astype(BF)

    def send_state(k, c):
        state_copy((me + k) % n, me).start()
        return c

    lax.fori_loop(1, n, send_state, 0)
    mine = pl.ds(pl.multiple_of(me * scap, scap), scap)
    st_recv[mine, :] = st_send[mine, :]
    ld_ws.wait()
    selfp[...] = dot(dot(qmat[...], newm[...]).astype(BF), ws[...])
    ld_wn.wait()

    def recv_state(k, c):
        s = (me - k + n) % n
        state_copy(s, s).wait_recv()
        return c

    lax.fori_loop(1, n, recv_state, 0)

    def rs_copy(j, to):
        return pltpu.make_async_remote_copy(
            src_ref=rs_send.at[j], dst_ref=rs_recv.at[j],
            send_sem=rs_ssem.at[j], recv_sem=rs_rsem.at[j],
            device_id=(me, to), device_id_type=MESH,
        )

    def embed(b0, b1):
        ats = [pl.ds(pl.multiple_of(b * qblock, qblock), qblock) for b in (b0, b1)]
        tally = jnp.concatenate([cmat[at, :] for at in ats], axis=0)
        mean = (dot(tally, st_recv[...]) / float(neigh_ref.shape[0])).astype(BF)
        out = dot(mean, wn[...])
        return out[:qblock] + selfp[ats[0], :], out[qblock:] + selfp[ats[1], :]

    to_core = [rs_copy(0, core), rs_copy(1, core)]
    to_cross = rs_copy(2, cross)
    part0, part1 = embed(far, core)
    rs_send[0] = part0.astype(BF)
    to_core[0].start()
    rs_send[1] = part1.astype(BF)
    to_core[1].start()
    part0, part1 = embed(cross, m)
    to_core[0].wait_recv()
    rs_send[2] = (part0 + rs_recv[0].astype(F32)).astype(BF)
    to_cross.start()
    to_core[1].wait_recv()
    part1 = part1 + rs_recv[1].astype(F32) + b_emb_ref[...]
    to_cross.wait_recv()
    emb_ref[...] = jnp.maximum(part1 + rs_recv[2].astype(F32), 0.0).astype(BF)

    def drain(s, c):
        relay(m, s, cross, xs_sem, xr_sem).wait_send()
        relay(m, s, core, c1s_sem, c1r_sem).wait_send()
        relay(cross, s, core, c2s_sem, c2r_sem).wait_send()
        return c

    lax.fori_loop(0, n, drain, 0)

    def drain_peers(k, c):
        d = (me + k) % n
        for cp in dispatch_copies(d, me):
            cp.wait_send()
        state_copy(d, me).wait_send()
        return c

    lax.fori_loop(1, n, drain_peers, 0)
    for cp in stage1 + stage2 + stage3 + to_core + [to_cross]:
        cp.wait_send()


def per_device(
    event_feats, event_owner, event_slot, memory, w_msg_event, w_msg_state, b_msg, w_msg_out,
    b_out, w_input, w_hidden, b_input, b_hidden, state_slots, neighbours, query_slots,
    w_neigh, w_self, b_embed,
):
    n = lax.axis_size("nodes")
    shares = lax.axis_size("mp")
    assert shares == 4
    events, feat = event_feats.shape
    nodes, width = memory.shape
    cap = 2 * events // n
    share = width // shares
    hid = w_msg_event.shape[1]
    half = width // 2
    scap = state_slots.shape[1]
    queries = query_slots.shape[0]
    qblock = queries // shares
    fcols = feat // shares
    vm = pl.BlockSpec(memory_space=pltpu.VMEM)
    hbm = pl.BlockSpec(memory_space=pl.ANY)
    V = pltpu.VMEM
    dma = lambda k: pltpu.SemaphoreType.DMA((k,))
    scratch = [
        V((1, events), jnp.int32), V((1, events), jnp.int32), V((1, hid), F32),
        V((1, width), F32), V(b_input.shape, F32), V(b_hidden.shape, F32),
        V(state_slots.shape, jnp.int32), V(neighbours.shape[::-1], jnp.int32),
        V((1, queries), jnp.int32), V((1, width), F32),
        V((events, fcols), BF), V(memory.shape, BF), V(w_msg_event.shape, BF),
        V(w_msg_state.shape, BF), V(w_msg_out.shape, BF), V(w_input.shape, BF),
        V(w_hidden.shape, BF), V(w_neigh.shape, BF), V(w_self.shape, BF),
        V((1, events), F32), V((events, LANES), BF), V((n, cap, fcols), BF),
        V((n, 1, cap), F32), V((4, n, cap, fcols), BF), V((n, 1, cap), F32),
        V((nodes, hid), BF), V((3, nodes, share), F32),
        V((nodes, hid), F32), V((nodes, LANES), F32),
        V((nodes, half), BF), V((nodes, half), BF), V((nodes, half), F32),
        V((nodes, half), BF), V((nodes, half), BF), V((nodes, half), BF), V((nodes, half), BF),
        V((n * scap, nodes), BF), V((queries, n * scap), BF), V((queries, nodes), BF),
        V((nodes, share), BF), V((n * scap, share), BF), V((n * scap, share), BF),
        V((queries, width), F32), V((3, qblock, width), BF), V((3, qblock, width), BF),
        dma(19), dma(n), dma(n), dma(n), dma(n), dma(n), dma(n),
        dma(n), dma(n), dma(n), dma(n), dma(3 * AR_CHUNKS), dma(3 * AR_CHUNKS), dma(n), dma(n), dma(3), dma(3),
    ]
    return pl.pallas_call(
        functools.partial(kernel, n),
        out_shape=(
            jax.ShapeDtypeStruct((nodes, share), BF),
            jax.ShapeDtypeStruct((qblock, width), BF),
        ),
        in_specs=[hbm] * 19,
        out_specs=(vm, vm),
        scratch_shapes=scratch,
        compiler_params=pltpu.CompilerParams(
            collective_id=0, has_side_effects=True, vmem_limit_bytes=VMEM_BYTES
        ),
        cost_estimate=pl.CostEstimate(flops=8_000_000_000, bytes_accessed=9_000_000, transcendentals=0),
    )(
        event_owner.reshape(1, events), event_slot.reshape(1, events), b_msg.reshape(1, -1),
        b_out.reshape(1, -1), b_input, b_hidden, state_slots, neighbours.T,
        query_slots.reshape(1, -1), b_embed.reshape(1, -1),
        event_feats, memory, w_msg_event, w_msg_state, w_msg_out, w_input, w_hidden,
        w_neigh, w_self,
    )

def solution(mesh):
    in_specs = (
        P("nodes", None),
        P("nodes", None),
        P("nodes"),
        P("nodes", None),
        P(None, "mp"),
        P(None, "mp"),
        P("mp"),
        P("mp", None),
        P(),
        P(None, None, "mp"),
        P(None, None, "mp"),
        P(None, "mp"),
        P(None, "mp"),
        P("nodes", None),
        P("nodes", None),
        P("nodes"),
        P("mp", None),
        P("mp", None),
        P(),
    )
    out_specs = (P("nodes", "mp"), P(("nodes", "mp"), None))
    return jax.shard_map(
        per_device, mesh=mesh, in_specs=in_specs, out_specs=out_specs, check_vma=False
    )
```
